256 devices in a mesh: row: 8 (over y, core), col: 16 (over z, x_hi), depth: 2 (over x_lo).
Axes of the slice: x: 4 (x_hi: 2, x_lo: 2; x = x_hi * 2 + x_lo), y: 4, z: 8, core: 2. Of those that a mesh axis runs over, the one named last changes fastest.
Arguments:
- a_blocks: float32 [192, 16, 128, 128], P('row', 'col'), may hold values from -6 to 6
- a_index: int32 [2, 192, 16], P(None, 'row', 'col'), may hold values from -1 to 383, as said below
- b_blocks: float32 [2, 64, 16, 128, 128], P(None, 'row', 'col'), may hold values from -0.5 to 0.5
- b_index: int32 [2, 2, 64, 16], P(None, None, 'row', 'col'), may hold values from -1 to 383, as said below
- c_index: int32 [2, 256, 16], P(None, 'row', 'col'), may hold values from -1 to 383, as said below
Outputs:
- c_blocks: float32 [256, 16, 128, 128], P('row', 'col')
The draws below stay inside these ranges and needn't reach their ends.
Inputs may be any that keep to these rules, and one draw needn't show every extreme that they name: `a_index`: A slot's two entries are both -1 (empty) or both live; a live slot of slot group r and column g names a block row of row group r (rows r * 48 to (r + 1) * 48 - 1) and an inner index of inner group g (g * 24 to (g + 1) * 24 - 1); no block is named twice; every group pair holds 12 to 24 live slots, and some pair holds 24. `b_index`: slots are both -1 or both live; a live slot of half h, slot group r, column c names an inner index of inner group h * 8 + r and a block column of column group c (c * 24 to (c + 1) * 24 - 1); no block is named twice; in every group pair at most 2 live blocks share one inner index, and in each pair some inner index is shared by exactly 2 live blocks. `c_index`: slots are both -1 or both live; a live slot of slot group r and column c names a block row of row group r and a block column of column group c; no block is named twice; every group pair holds 16 to 32 live slots, and some pair holds 32.
All inputs are finite; a program needn't handle non-finite values.
Results may differ from the reference program's by a relative error of at most 0.0003.
Values sent between devices are 32-bit elements; how exact they have to be, the bound alone decides.
A program may use at most 128 MiB of HBM per device.

```python
import jax
import jax.numpy as jnp
from jax import lax

BLK = 128
RACT = 12
KACT = 4
JACT = 6
MATCH = 2
A_CAP = 24
C_CAP = 32
ROW_SPAN = 48
INNER_SPAN = 24
B_HALF = 8
HALVES = 2
A_SLOTS = 192
B_SLOTS = 64
N_ROW = 8
N_COL = 16


def choose_live(subkey, span, count):
    return jax.random.permutation(subkey, span)[:count].astype(jnp.int32)


def active_sets(key):
    first, second, third = jax.random.split(key, 3)
    row_keys = jax.random.split(first, N_ROW)
    row_live = jax.vmap(lambda subkey: choose_live(subkey, ROW_SPAN, RACT))(row_keys)
    row_live = row_live + (jnp.arange(N_ROW, dtype=jnp.int32) * ROW_SPAN)[:, None]
    inner_keys = jax.random.split(second, N_COL)
    inner_live = jax.vmap(lambda subkey: choose_live(subkey, INNER_SPAN, KACT))(inner_keys)
    inner_live = inner_live + (jnp.arange(N_COL, dtype=jnp.int32) * INNER_SPAN)[:, None]
    col_keys = jax.random.split(third, N_COL)
    col_live = jax.vmap(lambda subkey: choose_live(subkey, INNER_SPAN, JACT))(col_keys)
    col_live = col_live + (jnp.arange(N_COL, dtype=jnp.int32) * INNER_SPAN)[:, None]
    return (row_live, inner_live, col_live)


def draw_a_index(key, part):
    row_live, inner_live, col_live = active_sets(key)
    key = jax.random.fold_in(key, 11)
    tiles = N_ROW * N_COL
    keys = jax.random.split(key, tiles + 1)
    full_tile = jax.random.randint(keys[tiles], (), 0, tiles)

    def one_tile(subkey, number):
        first, second = jax.random.split(subkey)
        cells = jax.random.permutation(first, RACT * KACT)[:A_CAP].astype(jnp.int32)
        count = jax.random.randint(second, (), A_CAP // 2, A_CAP + 1)
        count = jnp.where(number == full_tile, A_CAP, count)
        rows = row_live[number // N_COL][cells // KACT]
        inners = inner_live[number % N_COL][cells % KACT]
        usable = jnp.arange(A_CAP, dtype=jnp.int32) < count
        return jnp.stack([jnp.where(usable, rows, -1), jnp.where(usable, inners, -1)])
    lists = jax.vmap(one_tile)(keys[:tiles], jnp.arange(tiles, dtype=jnp.int32))
    lists = lists.reshape(N_ROW, N_COL, 2, A_CAP).transpose(2, 0, 3, 1)
    return lists.reshape(2, N_ROW * A_CAP, N_COL).astype(jnp.int32)


def draw_b_index(key, part):
    row_live, inner_live, col_live = active_sets(key)
    key = jax.random.fold_in(key, 23)
    tiles = N_COL * N_COL
    keys = jax.random.split(key, tiles)

    def one_tile(subkey, number):
        first, second, third = jax.random.split(subkey, 3)
        counts = jax.random.randint(first, (KACT,), 0, MATCH + 1)
        full_row = jax.random.randint(second, (), 0, KACT)
        counts = jnp.where(jnp.arange(KACT, dtype=jnp.int32) == full_row, MATCH, counts)
        picks = jax.vmap(lambda subkey: choose_live(subkey, JACT, MATCH))(jax.random.split(third, KACT))
        inners = jnp.broadcast_to(inner_live[number // N_COL][:, None], (KACT, MATCH))
        columns = col_live[number % N_COL][picks]
        usable = jnp.arange(MATCH, dtype=jnp.int32)[None, :] < counts[:, None]
        return jnp.stack([jnp.where(usable, inners, -1).reshape(-1), jnp.where(usable, columns, -1).reshape(-1)])
    lists = jax.vmap(one_tile)(keys, jnp.arange(tiles, dtype=jnp.int32))
    lists = lists.reshape(HALVES, N_ROW, N_COL, 2, B_HALF).transpose(3, 0, 1, 4, 2)
    return lists.reshape(2, HALVES, N_ROW * B_HALF, N_COL).astype(jnp.int32)


def draw_c_index(key, part):
    row_live, inner_live, col_live = active_sets(key)
    key = jax.random.fold_in(key, 37)
    tiles = N_ROW * N_COL
    keys = jax.random.split(key, tiles + 1)
    full_tile = jax.random.randint(keys[tiles], (), 0, tiles)

    def one_tile(subkey, number):
        first, second = jax.random.split(subkey)
        cells = jax.random.permutation(first, RACT * JACT)[:C_CAP].astype(jnp.int32)
        count = jax.random.randint(second, (), C_CAP // 2, C_CAP + 1)
        count = jnp.where(number == full_tile, C_CAP, count)
        rows = row_live[number // N_COL][cells // JACT]
        columns = col_live[number % N_COL][cells % JACT]
        usable = jnp.arange(C_CAP, dtype=jnp.int32) < count
        return jnp.stack([jnp.where(usable, rows, -1), jnp.where(usable, columns, -1)])
    lists = jax.vmap(one_tile)(keys[:tiles], jnp.arange(tiles, dtype=jnp.int32))
    lists = lists.reshape(N_ROW, N_COL, 2, C_CAP).transpose(2, 0, 3, 1)
    return lists.reshape(2, N_ROW * C_CAP, N_COL).astype(jnp.int32)


def levels(key, shape, cuts, least, largest):
    loudness = 1.0
    for position, parts in cuts:
        heights = jax.random.uniform(jax.random.fold_in(jax.random.fold_in(key, 6), position), (parts,), jnp.float32, least / len(cuts), largest / len(cuts))
        loudness = loudness * jnp.repeat(jnp.exp(heights), shape[position] // parts).reshape((-1,) + (1,) * (len(shape) - 1 - position))
    return loudness


def gaussian(own_key, extent, deviation, bound, cuts=(), held_as=jnp.bfloat16):
    level = levels(own_key, extent, cuts, -0.22, 0.18) if cuts else 1.0
    values = jax.random.normal(own_key, extent, jnp.float32) * deviation * level
    return jnp.minimum(jnp.maximum(values, -bound), bound).astype(held_as)


def setup_inputs(seed: int = 0) -> dict:
    streams_of = jax.random.split(jax.random.key(seed), 6)
    return {
        "a_blocks": gaussian(streams_of[0], (A_SLOTS, N_COL, BLK, BLK), 1.0, 6.0, ((0, 8), (1, 16)), jnp.float32),
        "a_index": draw_a_index(jax.random.fold_in(streams_of[5], 71), 0),
        "b_blocks": gaussian(streams_of[2], (HALVES, B_SLOTS, N_COL, BLK, BLK), BLK ** -0.5, 0.5, ((1, 8), (2, 16)), jnp.float32),
        "b_index": draw_b_index(jax.random.fold_in(streams_of[5], 71), 0),
        "c_index": draw_c_index(jax.random.fold_in(streams_of[5], 71), 0),
    }


PRECISE = lax.Precision.HIGHEST


def tile_product(partial_value, row_tiles, row_ids, inner_ids, col_tiles, inner_keys, col_ids, out_rows, out_cols):
    pairing = (inner_ids[:, None] == inner_keys[None, :]) & (inner_ids[:, None] >= 0)
    ranking = (jnp.cumsum(pairing.astype(jnp.int32), axis=1) - 1).astype(jnp.int32)
    positions = jnp.arange(MATCH, dtype=jnp.int32)
    chooser = pairing[:, None, :] & (ranking[:, None, :] == positions[None, :, None])
    one_hot = chooser.astype(jnp.float32)
    gathered = jnp.einsum("amb,bxy->amxy", one_hot, col_tiles.astype(jnp.float32), precision=PRECISE)
    target = jnp.sum(jnp.where(chooser, col_ids[None, None, :], 0), axis=2).astype(jnp.int32)
    usable = jnp.any(chooser, axis=2)
    products = jnp.einsum("axy,amyz->amxz", row_tiles.astype(jnp.float32), gathered, precision=PRECISE)
    routing = (out_rows[:, None, None] == row_ids[None, :, None]) & (out_cols[:, None, None] == target[None, :, :])
    routing = routing & usable[None, :, :] & (out_rows[:, None, None] >= 0)
    return partial_value + jnp.einsum("cam,amxz->cxz", routing.astype(jnp.float32), products, precision=PRECISE)


def reference(a_blocks, a_index, b_blocks, b_index, c_index):
    def one_tile(tile_number):
        band_row = tile_number // N_COL
        band_col = tile_number % N_COL
        out_rows = lax.dynamic_index_in_dim(lax.dynamic_slice_in_dim(c_index[0], band_row * C_CAP, C_CAP, 0), band_col, 1, False)
        out_cols = lax.dynamic_index_in_dim(lax.dynamic_slice_in_dim(c_index[1], band_row * C_CAP, C_CAP, 0), band_col, 1, False)
        a_band = lax.dynamic_slice_in_dim(a_blocks, band_row * A_CAP, A_CAP, 0)
        a_rows_band = lax.dynamic_slice_in_dim(a_index[0], band_row * A_CAP, A_CAP, 0)
        a_cols_band = lax.dynamic_slice_in_dim(a_index[1], band_row * A_CAP, A_CAP, 0)

        def section(partial_value, inner_group):
            row_tiles = lax.dynamic_index_in_dim(a_band, inner_group, 1, False)
            row_ids = lax.dynamic_index_in_dim(a_rows_band, inner_group, 1, False)
            inner_ids = lax.dynamic_index_in_dim(a_cols_band, inner_group, 1, False)
            half_index = inner_group // N_ROW
            start = (inner_group % N_ROW) * B_HALF
            b_half = lax.dynamic_index_in_dim(b_blocks, half_index, 0, False)
            col_tiles = lax.dynamic_index_in_dim(lax.dynamic_slice_in_dim(b_half, start, B_HALF, 0), band_col, 1, False)
            keys_half = lax.dynamic_index_in_dim(b_index[0], half_index, 0, False)
            cols_half = lax.dynamic_index_in_dim(b_index[1], half_index, 0, False)
            inner_keys = lax.dynamic_index_in_dim(lax.dynamic_slice_in_dim(keys_half, start, B_HALF, 0), band_col, 1, False)
            col_ids = lax.dynamic_index_in_dim(lax.dynamic_slice_in_dim(cols_half, start, B_HALF, 0), band_col, 1, False)
            partial_value = tile_product(partial_value, row_tiles, row_ids, inner_ids, col_tiles, inner_keys, col_ids, out_rows, out_cols)
            return partial_value, None

        start_value = jnp.zeros((C_CAP, BLK, BLK), jnp.float32)
        result, unused = lax.scan(section, start_value, jnp.arange(N_COL, dtype=jnp.int32))
        return result

    tiles = lax.map(one_tile, jnp.arange(N_ROW * N_COL, dtype=jnp.int32))
    tiles = tiles.reshape(N_ROW, N_COL, C_CAP, BLK, BLK).transpose(0, 2, 1, 3, 4)
    return tiles.reshape(N_ROW * C_CAP, N_COL, BLK, BLK)
```

```python
import functools

import jax
import jax.numpy as jnp
from jax import lax
from jax.experimental import pallas as pl
from jax.experimental.pallas import tpu as pltpu
from jax.sharding import PartitionSpec as P

MESH = pl.DeviceIdType.MESH
NZ, NY = 8, 4
ASLOT, BSLOT, CSLOT, BLK = 24, 8, 32, 128
ROWS = BLK // 2
PARTS, PSLOT = 4, ASLOT // 4
CCH, CSZ = 4, CSLOT // 4
LANE_A = 32
ZERO = 2 * ASLOT


def kernel(
    idx_ref, a_ref, b_ref, o_ref,
    idx_a, idx_b, idx_c, tab_v, low_v, tab_s, low_s,
    abuf, bbuf, bhi, blo, prods, acc, crecv,
    s_ia, r_ia, s_ib, r_ib, s_ic, r_ic, s_tab,
    s_al, s_ar, r_a, s_loc, s_bd, s_bf, s_bx, r_b, s_c, r_c, s_o, s_m, r_m,
):
    r = lax.axis_index("row")
    c = lax.axis_index("col")
    d = lax.axis_index("depth")
    y, q = r // 2, r % 2
    z, h = c // 2, c % 2
    half = (h + d) % 2
    own = q == h
    b_col = z * 2 + q
    b_depth = (d + h + q) % 2
    partner = (r, z * 2 + 1 - h, 1 - d)
    mate = (r, c, 1 - d)
    twin = (y * 2 + 1 - q, c, d)
    up, down = (((y + 1) % NY) * 2 + q, c, d), (((y + 3) % NY) * 2 + q, c, d)
    right, left = (r, ((z + 1) % NZ) * 2 + h, d), (r, ((z + 7) % NZ) * 2 + h, d)

    def remote(src, dst, send, recv, device):
        return pltpu.make_async_remote_copy(
            src_ref=src, dst_ref=dst, send_sem=send, recv_sem=recv, device_id=device, device_id_type=MESH
        )

    def landed(ref, sem):
        pltpu.make_async_copy(ref, ref, sem).wait()

    barrier = pltpu.get_barrier_semaphore()

    def greet(device):
        pl.semaphore_signal(barrier, inc=1, device_id=device, device_id_type=MESH)

    def greet_z(i, carry):
        greet((r, ((z + i) % NZ) * 2 + h, d))
        return carry

    lax.fori_loop(1, NZ, greet_z, 0)

    def greet_b(i, carry):
        yy = (y + i) % NY
        greet((yy * 2 + h, z * 2 + 1 - h, 1 - d))

        @pl.when(jnp.logical_not(own & (i == 0)))
        def _():
            greet((yy * 2 + h, c, d))

        return carry

    lax.fori_loop(0, NY, greet_b, 0)
    for device in (partner, mate, twin, up, down):
        greet(device)
    pl.semaphore_wait(barrier, NZ - 1 + 2 * NY + 5 - own.astype(jnp.int32))

    def send_ia(i):
        return remote(idx_ref, idx_a.at[z], s_ia.at[i], r_ia.at[z], (r, ((z + i) % NZ) * 2 + h, d))

    def send_ib(i):
        yy, core = (y + i // 2) % NY, i % 2
        return remote(idx_ref, idx_b.at[h * NY + y], s_ib.at[i], r_ib.at[h * NY + y], (yy * 2 + core, b_col, b_depth))

    def other_ib(i):
        return jnp.logical_not(own & (i // 2 == 0) & (i % 2 == q))

    send_ic = remote(idx_ref, idx_c, s_ic, r_ic, partner)

    def start_ia(i, carry):
        send_ia(i).start()
        return carry

    def start_ib(i, carry):
        pl.when(other_ib(i))(lambda: send_ib(i).start())
        return carry

    lax.fori_loop(1, NZ, start_ia, 0)
    lax.fori_loop(0, 2 * NY, start_ib, 0)
    send_ic.start()

    def send_bd(i, s):
        yy = (y + i) % NY
        return remote(
            b_ref.at[s, :, 0], bbuf.at[h, s * NY + y], s_bd.at[i, s], r_b.at[h, s * NY + y], (yy * 2 + s, b_col, b_depth)
        )

    local_b = pltpu.make_async_copy(b_ref.at[q, :, 0], bbuf.at[h, q * NY + y], r_b.at[h, q * NY + y])
    for i in (0, 1, 3):
        for s in (0, 1):
            if i:
                send_bd(i, s).start()
            else:
                pl.when(jnp.logical_not(own & (q == s)))(lambda: send_bd(0, s).start())
    pl.when(own)(local_b.start)

    def own_part(p):
        return a_ref.at[pl.ds(p * PSLOT, PSLOT), 0, pl.ds(half * ROWS, ROWS), :]

    def part(zz, p):
        return abuf.at[zz, pl.ds(p * PSLOT, PSLOT)]

    def a_right(dist, p):
        zz = (z + NZ - dist) % NZ
        return remote(part(zz, p), part(zz, p), s_ar.at[dist, p], r_a.at[zz, p], right)

    def a_left(dist, p):
        zz = (z + dist) % NZ
        return remote(part(zz, p), part(zz, p), s_al.at[dist, p], r_a.at[zz, p], left)

    local_a = pltpu.make_async_copy(a_ref.at[:, 0, pl.ds(half * ROWS, ROWS), :], abuf.at[z], s_loc)

    def start_a(p, carry):
        remote(own_part(p), part(z, p), s_ar.at[0, p], r_a.at[z, p], right).start()
        remote(own_part(p), part(z, p), s_al.at[0, p], r_a.at[z, p], left).start()
        return carry

    lax.fori_loop(0, PARTS, start_a, 0)
    local_a.start()

    idx_a[z] = idx_ref[...]

    @pl.when(own)
    def _():
        idx_b[h * NY + y] = idx_ref[...]

    acc[...] = jnp.zeros_like(acc)
    prods[0, ZERO] = jnp.zeros((ROWS, BLK), jnp.float32)
    prods[1, ZERO] = jnp.zeros((ROWS, BLK), jnp.float32)

    def wait_ia(i, carry):
        zz = (z + i) % NZ
        landed(idx_a.at[zz], r_ia.at[zz])
        return carry

    lax.fori_loop(1, NZ, wait_ia, 0)

    def wait_ib(i, carry):
        yy = (y + i) % NY
        landed(idx_b.at[(1 - h) * NY + yy], r_ib.at[(1 - h) * NY + yy])
        pl.when(jnp.logical_not(own & (i == 0)))(lambda: landed(idx_b.at[h * NY + yy], r_ib.at[h * NY + yy]))
        return carry

    lax.fori_loop(0, NY, wait_ib, 0)
    landed(idx_c, r_ic)

    a_all = jnp.sum(idx_a[...], axis=0)
    b_all = jnp.sum(idx_b[...], axis=0)
    a_row, a_in = a_all[0:1], a_all[1:2]
    b_key, b_to = b_all[2:3, :BLK], b_all[3:4, :BLK]

    def column(row, count):
        wide = jnp.broadcast_to(row, (count, BLK))
        at = lax.broadcasted_iota(jnp.int32, (count, BLK), 0)
        lane = lax.broadcasted_iota(jnp.int32, (count, BLK), 1)
        return jnp.sum(jnp.where(at == lane, wide, 0), axis=1, keepdims=True)

    key_col = column(b_key, BLK)
    at = lax.broadcasted_iota(jnp.int32, (BLK, 2 * BLK), 0)
    match = (key_col == a_in) & (a_in > 0)
    low_v[...] = jnp.zeros_like(low_v)
    for cp in (0, 1):
        mine = match & (at // (BLK // 2) == cp)
        first = jnp.min(jnp.where(mine, at % BSLOT, BSLOT), axis=0, keepdims=True)
        last = jnp.max(jnp.where(mine, at % BSLOT, 0), axis=0, keepdims=True)
        low_v[2 * cp : 2 * cp + 1] = jnp.where(first == BSLOT, 0, first)
        low_v[2 * cp + 1 : 2 * cp + 2] = last
    at2 = at[:, :BLK]
    lane2 = lax.broadcasted_iota(jnp.int32, (BLK, BLK), 1)
    earlier = (key_col == b_key) & (at2 < lane2) & (at2 // (BLK // 2) == lane2 // (BLK // 2))
    second = jnp.max(jnp.where(earlier, 1, 0), axis=0, keepdims=True)
    row_col = jnp.concatenate([column(a_row[:, :BLK], BLK), column(a_row[:, BLK:], BLK)], axis=0)
    in_col = jnp.concatenate([column(a_in[:, :BLK], BLK), column(a_in[:, BLK:], BLK)], axis=0)
    slot = lax.broadcasted_iota(jnp.int32, (2 * BLK, BLK), 0) % LANE_A
    weight = jnp.where((in_col == b_key) & (in_col > 0), slot + 1, 0)
    mine_c, other_c = idx_ref[...], idx_c[...]
    lane3 = lax.broadcasted_iota(jnp.int32, (CSLOT, BLK), 1)
    low_half = lane3 < BLK // 2
    at_zero = jnp.where(h == 0, mine_c, other_c)
    at_one = jnp.where(h == 0, other_c, mine_c)
    tab_v[0] = jnp.where(low_half, column(at_zero[4:5, :BLK], CSLOT), column(at_one[4:5, :BLK], CSLOT))
    tab_v[1] = jnp.where(low_half, column(at_zero[5:6, :BLK], CSLOT), column(at_one[5:6, :BLK], CSLOT))

    def one_slot(s, carry):
        out_row, out_col = tab_v[0, pl.ds(s, 1)], tab_v[1, pl.ds(s, 1)]
        found = jnp.max(jnp.where(row_col == out_row, weight, 0), axis=0, keepdims=True)
        place = jnp.clip(2 * found - 2 + second, 0, ZERO)
        tab_v[2, pl.ds(s, 1)] = jnp.where((found > 0) & (out_col == b_to), place, ZERO)
        return carry

    lax.fori_loop(0, CSLOT, one_slot, 0)
    tab_copy = pltpu.make_async_copy(tab_v.at[2], tab_s, s_tab.at[0])
    low_copy = pltpu.make_async_copy(low_v, low_s, s_tab.at[1])
    tab_copy.start()
    low_copy.start()
    tab_copy.wait()
    low_copy.wait()

    def spread(cp, zz, slot):
        return remote(bbuf.at[cp, zz], bbuf.at[cp, zz], s_bx.at[slot], r_b.at[cp, zz], twin)

    def split_b(cp, zz):
        def one(i, carry):
            value = bbuf[cp, zz, i]
            high = value.astype(jnp.bfloat16)
            bhi[cp, zz, i] = high
            blo[cp, zz, i] = (value - high.astype(jnp.float32)).astype(jnp.bfloat16)
            return carry

        lax.fori_loop(0, BSLOT, one, 0)

    def b_here(i, cp):
        zz = q * NY + (y + i) % NY
        landed(bbuf.at[cp, zz], r_b.at[cp, zz])
        spread(cp, zz, i * 2 + cp).start()

    def b_pass(cp):
        zz = q * NY + (y + (3 if cp == 0 else 1)) % NY
        return remote(bbuf.at[cp, zz], bbuf.at[cp, zz], s_bf.at[cp], r_b.at[cp, zz], up if cp == 0 else down)

    def a_step(dist):
        def one(p, carry):
            landed(part((z + NZ - dist) % NZ, p), r_a.at[(z + NZ - dist) % NZ, p])
            a_right(dist, p).start()
            landed(part((z + dist) % NZ, p), r_a.at[(z + dist) % NZ, p])
            a_left(dist, p).start()
            return carry

        lax.fori_loop(0, PARTS, one, 0)

    b_here(0, 0)
    b_here(0, 1)
    a_step(1)
    b_here(3, 0)
    b_pass(0).start()
    b_here(1, 1)
    b_pass(1).start()
    b_here(3, 1)
    b_here(1, 0)
    a_step(2)
    b_here(2, 0)
    b_here(2, 1)

    def take_b(i, carry):
        cp, zz = i // NZ, i % NZ

        @pl.when(zz // NY != q)
        def _():
            landed(bbuf.at[cp, zz], r_b.at[cp, zz])

        split_b(cp, zz)
        return carry

    lax.fori_loop(0, 2 * NZ, take_b, 0)
    local_a.wait()

    def group(k, carry):
        step = (k + 1) // 2
        zz = (z + NZ + jnp.where(k % 2 == 1, step, -step)) % NZ
        far_l, far_r = (z + NZ - 3) % NZ, (z + 3) % NZ

        @pl.when(k < PARTS)
        def _():
            landed(part(far_l, k), r_a.at[far_l, k])
            pl.when(k < PARTS // 2)(lambda: a_right(3, k).start())
            landed(part(far_r, k), r_a.at[far_r, k])
            pl.when(k >= PARTS // 2)(lambda: a_left(3, k).start())

        @pl.when(k == NZ - 1)
        def _():
            for p in range(PARTS):
                landed(part(zz, p), r_a.at[zz, p])

        def multiply(a, carry):
            value = abuf[zz, a]
            high = value.astype(jnp.bfloat16)
            low = (value - high.astype(jnp.float32)).astype(jnp.bfloat16)
            both = jnp.concatenate([high, low], axis=0)
            for o in (0, 1):
                cp = h if o == 0 else 1 - h
                b0 = low_s[2 * cp, zz * LANE_A + a]
                b1 = low_s[2 * cp + 1, zz * LANE_A + a]
                wide = jnp.concatenate([bhi[cp, zz, b0], bhi[cp, zz, b1]], axis=1)
                fine = jnp.concatenate([blo[cp, zz, b0], blo[cp, zz, b1]], axis=1)
                big = jnp.dot(both, wide, preferred_element_type=jnp.float32)
                small = jnp.dot(high, fine, preferred_element_type=jnp.float32)
                total = big[:ROWS] + (big[ROWS:] + small)
                prods[o, 2 * a] = total[:, :BLK]
                prods[o, 2 * a + 1] = total[:, BLK:]
            return carry

        lax.fori_loop(0, ASLOT, multiply, 0)

        def gather(s, carry):
            for o in (0, 1):
                cp = h if o == 0 else 1 - h
                base = cp * (BLK // 2) + zz * BSLOT
                terms = [prods[o, tab_s[s, base + b]] for b in range(BSLOT)]
                while len(terms) > 1:
                    terms = [x + w for x, w in zip(terms[::2], terms[1::2])]
                acc[o, s] += terms[0]
            return carry

        lax.fori_loop(0, CSLOT, gather, 0)
        return carry

    lax.fori_loop(0, NZ, group, 0)

    def c_piece(o, j):
        return acc.at[o, pl.ds(j * CSZ, CSZ)]

    def send_c(j):
        return remote(c_piece(1, j), crecv.at[pl.ds(j * CSZ, CSZ)], s_c.at[j], r_c.at[j], partner)

    def out_piece(j, which):
        return o_ref.at[pl.ds(j * CSZ, CSZ), 0, pl.ds(which * ROWS, ROWS), :]

    def send_m(j):
        return remote(c_piece(0, j), out_piece(j, half), s_m.at[j], r_m.at[j], mate)

    def store_o(j):
        return pltpu.make_async_copy(c_piece(0, j), out_piece(j, half), s_o.at[j])

    for j in range(CCH):
        send_c(j).start()
    for j in range(CCH):
        landed(crecv.at[pl.ds(j * CSZ, CSZ)], r_c.at[j])

        def add(s, carry):
            acc[0, s] += crecv[s]
            return carry

        lax.fori_loop(j * CSZ, (j + 1) * CSZ, add, 0)
        send_m(j).start()
        store_o(j).start()

    for j in range(CCH):
        landed(out_piece(j, 1 - half), r_m.at[j])
        store_o(j).wait()
        send_m(j).wait_send()
        send_c(j).wait_send()

    def end_ia(i, carry):
        send_ia(i).wait_send()
        return carry

    def end_ib(i, carry):
        pl.when(other_ib(i))(lambda: send_ib(i).wait_send())
        return carry

    lax.fori_loop(1, NZ, end_ia, 0)
    lax.fori_loop(0, 2 * NY, end_ib, 0)
    send_ic.wait_send()
    for i in (0, 1, 3):
        for s in (0, 1):
            if i:
                send_bd(i, s).wait_send()
            else:
                pl.when(jnp.logical_not(own & (q == s)))(lambda: send_bd(0, s).wait_send())
    for cp in (0, 1):
        b_pass(cp).wait_send()
        for i in range(NY):
            spread(cp, q * NY + (y + i) % NY, i * 2 + cp).wait_send()

    def end_a(p, carry):
        for dist in range(3):
            a_right(dist, p).wait_send()
            a_left(dist, p).wait_send()
        pl.when(p < PARTS // 2)(lambda: a_right(3, p).wait_send())
        pl.when(p >= PARTS // 2)(lambda: a_left(3, p).wait_send())
        return carry

    lax.fori_loop(0, PARTS, end_a, 0)


def index_rows(a_index, b_index, c_index):
    y = lax.axis_index("row") // 2
    z, h = lax.axis_index("col") // 2, lax.axis_index("col") % 2
    wide = jnp.zeros((8, 2 * BLK), jnp.int32)
    wide = lax.dynamic_update_slice(wide, a_index[:, :, 0] + 1, (0, z * LANE_A))
    for s in (0, 1):
        wide = lax.dynamic_update_slice(wide, b_index[:, s, :, 0] + 1, (2, h * (BLK // 2) + (s * NY + y) * BSLOT))
    return lax.dynamic_update_slice(wide, c_index[:, :, 0] + 1, (4, 0))


def local(a_blocks, a_index, b_blocks, b_index, c_index):
    dma = pltpu.SemaphoreType.DMA
    f32, bf16, i32 = jnp.float32, jnp.bfloat16, jnp.int32
    anywhere = pl.BlockSpec(memory_space=pl.ANY)
    return pl.pallas_call(
        kernel,
        out_shape=jax.ShapeDtypeStruct((CSLOT, 1, BLK, BLK), f32),
        in_specs=[pl.BlockSpec(memory_space=pltpu.VMEM), anywhere, anywhere],
        out_specs=anywhere,
        scratch_shapes=[
            pltpu.VMEM((NZ, 8, 2 * BLK), i32),
            pltpu.VMEM((2 * NY, 8, 2 * BLK), i32),
            pltpu.VMEM((8, 2 * BLK), i32),
            pltpu.VMEM((3, CSLOT, BLK), i32),
            pltpu.VMEM((8, 2 * BLK), i32),
            pltpu.SMEM((CSLOT, BLK), i32),
            pltpu.SMEM((8, 2 * BLK), i32),
            pltpu.VMEM((NZ, ASLOT, ROWS, BLK), f32),
            pltpu.VMEM((2, NZ, BSLOT, BLK, BLK), f32),
            pltpu.VMEM((2, NZ, BSLOT, BLK, BLK), bf16),
            pltpu.VMEM((2, NZ, BSLOT, BLK, BLK), bf16),
            pltpu.VMEM((2, ZERO + 1, ROWS, BLK), f32),
            pltpu.VMEM((2, CSLOT, ROWS, BLK), f32),
            pltpu.VMEM((CSLOT, ROWS, BLK), f32),
            dma((NZ,)), dma((NZ,)), dma((2 * NY,)), dma((2 * NY,)), dma, dma, dma((2,)),
            dma((4, PARTS)), dma((4, PARTS)), dma((NZ, PARTS)), dma,
            dma((NY, 2)), dma((2,)), dma((2 * NY,)), dma((2, NZ)),
            dma((CCH,)), dma((CCH,)), dma((CCH,)), dma((CCH,)), dma((CCH,)),
        ],
        compiler_params=pltpu.CompilerParams(
            collective_id=0, has_side_effects=True, vmem_limit_bytes=56 * 1024 * 1024
        ),
        cost_estimate=pl.CostEstimate(flops=10**10, bytes_accessed=10**7, transcendentals=0),
    )(index_rows(a_index, b_index, c_index), a_blocks, b_blocks)


def solution(mesh):
    in_specs = (
        P("row", "col", None, None),
        P(None, "row", "col"),
        P(None, "row", "col", None, None),
        P(None, None, "row", "col"),
        P(None, "row", "col"),
    )
    out_specs = P("row", "col", None, None)
    return jax.shard_map(local, mesh=mesh, in_specs=in_specs, out_specs=out_specs, check_vma=False)
```

```python
import functools

import jax
import jax.numpy as jnp
from jax import lax
from jax.experimental import pallas as pl
from jax.experimental.pallas import tpu as pltpu
from jax.sharding import PartitionSpec as P

MESH = pl.DeviceIdType.MESH
NZ, NY = 8, 4
ASLOT, BSLOT, CSLOT, BLK = 24, 8, 32, 128
ROWS = BLK // 2
PARTS, PROW = 4, ROWS // 4
SPANS, SROW = 2, ROWS // 2
CCH, CSZ = 4, CSLOT // 4
LANE_A = 32
ZERO = 2 * ASLOT


def kernel(
    idx_ref, a_ref, b_ref, o_ref,
    idx_a, idx_b, idx_c, tab_v, low_v, tab_s, low_s,
    abuf, bbuf, bhi, blo, prods, acc, crecv,
    s_ia, r_ia, s_ib, r_ib, s_ic, r_ic, s_tab,
    s_al, s_ar, r_a, s_loc, s_bd, s_bn, s_bf, s_bx, r_b, s_c, r_c, s_o, s_m, r_m,
):
    r = lax.axis_index("row")
    c = lax.axis_index("col")
    d = lax.axis_index("depth")
    y, q = r // 2, r % 2
    z, h = c // 2, c % 2
    half = (h + d) % 2
    own = q == h
    role = (q + h) % 2
    b_col = z * 2 + q
    b_depth = (d + h + q) % 2
    partner = (r, z * 2 + 1 - h, 1 - d)
    mate = (r, c, 1 - d)
    twin = (y * 2 + 1 - q, c, d)
    up, down = (((y + 1) % NY) * 2 + q, c, d), (((y + 3) % NY) * 2 + q, c, d)
    right, left = (r, ((z + 1) % NZ) * 2 + h, d), (r, ((z + 7) % NZ) * 2 + h, d)

    def remote(src, dst, send, recv, device):
        return pltpu.make_async_remote_copy(
            src_ref=src, dst_ref=dst, send_sem=send, recv_sem=recv, device_id=device, device_id_type=MESH
        )

    def landed(ref, sem):
        pltpu.make_async_copy(ref, ref, sem).wait()

    barrier = pltpu.get_barrier_semaphore()

    def greet(device):
        pl.semaphore_signal(barrier, inc=1, device_id=device, device_id_type=MESH)

    def greet_z(i, carry):
        greet((r, ((z + i) % NZ) * 2 + h, d))
        return carry

    lax.fori_loop(1, NZ, greet_z, 0)

    def greet_b(i, carry):
        yy = (y + i) % NY
        greet((yy * 2 + h, z * 2 + 1 - h, 1 - d))

        @pl.when(jnp.logical_not(own & (i == 0)))
        def _():
            greet((yy * 2 + h, c, d))

        return carry

    lax.fori_loop(0, NY, greet_b, 0)
    for device in (partner, mate, twin, up, down):
        greet(device)
    pl.semaphore_wait(barrier, NZ - 1 + 2 * NY + 5 - own.astype(jnp.int32))

    def send_bd(i, s):
        yy = (y + i) % NY
        return remote(b_ref.at[s, :, 0], bbuf.at[0, s * NY + y], s_bd.at[i, s], r_b.at[0, s * NY + y], (yy * 2 + s, c, d))

    def send_bp(s):
        return remote(
            b_ref.at[s, :, 0], bbuf.at[1, s * NY + y], s_bd.at[0, s], r_b.at[1, s * NY + y],
            (y * 2 + s, z * 2 + 1 - h, 1 - d),
        )

    local_b = pltpu.make_async_copy(b_ref.at[q, :, 0], bbuf.at[0, q * NY + y], r_b.at[0, q * NY + y])

    @pl.when(own)
    def _():
        for s in (0, 1):
            pl.when(q != s)(lambda: send_bd(0, s).start())
            send_bd(1, s).start()
            send_bd(3, s).start()
        local_b.start()

    @pl.when(jnp.logical_not(own))
    def _():
        send_bp(0).start()
        send_bp(1).start()

    def own_part(p):
        return a_ref.at[:, 0, pl.ds(half * ROWS + p * PROW, PROW), :]

    def part(zz, p):
        return abuf.at[zz, p]

    def turn(j):
        return j + 1 - 2 * (j % 2)

    def a_right(dist, j):
        zz = (z + NZ - dist) % NZ
        return remote(part(zz, j), part(zz, j), s_ar.at[dist, j], r_a.at[zz, j], right)

    def a_left(dist, j):
        zz, p = (z + dist) % NZ, turn(j)
        return remote(part(zz, p), part(zz, p), s_al.at[dist, j], r_a.at[zz, p], left)

    def from_left(dist, j):
        zz = (z + NZ - dist) % NZ
        landed(part(zz, j), r_a.at[zz, j])

    def from_right(dist, j):
        zz, p = (z + dist) % NZ, turn(j)
        landed(part(zz, p), r_a.at[zz, p])

    def local_a(p):
        return pltpu.make_async_copy(own_part(p), part(z, p), s_loc.at[p])

    def start_a(j, carry):
        p = turn(j)
        remote(own_part(j), part(z, j), s_ar.at[0, j], r_a.at[z, j], right).start()
        remote(own_part(p), part(z, p), s_al.at[0, j], r_a.at[z, p], left).start()
        local_a(j).start()
        return carry

    lax.fori_loop(0, PARTS, start_a, 0)

    def send_ia(i):
        return remote(idx_ref, idx_a.at[z], s_ia.at[i], r_ia.at[z], (r, ((z + i) % NZ) * 2 + h, d))

    def send_ib(i):
        yy, core = (y + i // 2) % NY, i % 2
        at = role * NY + y
        return remote(idx_ref, idx_b.at[at], s_ib.at[i], r_ib.at[at], (yy * 2 + core, b_col, b_depth))

    def other_ib(i):
        return jnp.logical_not(own & (i // 2 == 0) & (i % 2 == q))

    send_ic = remote(idx_ref, idx_c, s_ic, r_ic, partner)

    def start_ia(i, carry):
        send_ia(i).start()
        return carry

    def start_ib(i, carry):
        pl.when(other_ib(i))(lambda: send_ib(i).start())
        return carry

    lax.fori_loop(1, NZ, start_ia, 0)
    lax.fori_loop(0, 2 * NY, start_ib, 0)
    send_ic.start()
    idx_a[z] = idx_ref[...]

    @pl.when(own)
    def _():
        idx_b[y] = idx_ref[...]

    acc[...] = jnp.zeros_like(acc)
    for v in range(SPANS):
        for o in (0, 1):
            prods[v, o, ZERO] = jnp.zeros((SROW, BLK), jnp.float32)

    def tables():
        def wait_ia(i, carry):
            zz = (z + i) % NZ
            landed(idx_a.at[zz], r_ia.at[zz])
            return carry

        lax.fori_loop(1, NZ, wait_ia, 0)

        def wait_ib(i, carry):
            yy = (y + i) % NY
            landed(idx_b.at[NY + yy], r_ib.at[NY + yy])
            pl.when(jnp.logical_not(own & (i == 0)))(lambda: landed(idx_b.at[yy], r_ib.at[yy]))
            return carry

        lax.fori_loop(0, NY, wait_ib, 0)
        landed(idx_c, r_ic)

        a_sets = []
        for g in (0, 1):
            rolled = [pltpu.roll(idx_a[g * 4 + i] + 1, i * LANE_A, 1) if i else idx_a[g * 4] + 1 for i in range(4)]
            a_sets.append(rolled[0] + rolled[1] + (rolled[2] + rolled[3]))
        rolled = [pltpu.roll(idx_b[i] + 1, (i // NY) * (BLK // 2) + (i % NY) * BSLOT, 1) if i else idx_b[0] + 1 for i in range(2 * NY)]
        while len(rolled) > 1:
            rolled = [x + w for x, w in zip(rolled[::2], rolled[1::2])]
        b_key, b_to = rolled[0][2:3], rolled[0][3:4]
        a_in = jnp.concatenate([a_sets[0][1:2], a_sets[1][1:2]], axis=1)

        def column(row, count):
            wide = jnp.broadcast_to(row, (count, BLK))
            at = lax.broadcasted_iota(jnp.int32, (count, BLK), 0)
            lane = lax.broadcasted_iota(jnp.int32, (count, BLK), 1)
            return jnp.sum(jnp.where(at == lane, wide, 0), axis=1, keepdims=True)

        key_col = column(b_key, BLK)
        at = lax.broadcasted_iota(jnp.int32, (BLK, 2 * BLK), 0)
        match = (key_col == a_in) & (a_in > 0)
        low_v[...] = jnp.zeros_like(low_v)
        for o in (0, 1):
            mine = match & (at // (BLK // 2) == o)
            first = jnp.min(jnp.where(mine, at % BSLOT, BSLOT), axis=0, keepdims=True)
            last = jnp.max(jnp.where(mine, at % BSLOT, 0), axis=0, keepdims=True)
            low_v[2 * o : 2 * o + 1] = jnp.where(first == BSLOT, 0, first)
            low_v[2 * o + 1 : 2 * o + 2] = last
        at2 = at[:, :BLK]
        lane2 = lax.broadcasted_iota(jnp.int32, (BLK, BLK), 1)
        earlier = (key_col == b_key) & (at2 < lane2) & (at2 // (BLK // 2) == lane2 // (BLK // 2))
        second = jnp.max(jnp.where(earlier, 1, 0), axis=0, keepdims=True)
        row_col = jnp.concatenate([column(a_sets[g][0:1], BLK) for g in (0, 1)], axis=0)
        in_col = jnp.concatenate([column(a_sets[g][1:2], BLK) for g in (0, 1)], axis=0)
        slot = lax.broadcasted_iota(jnp.int32, (2 * BLK, BLK), 0) % LANE_A
        weight = jnp.where((in_col == b_key) & (in_col > 0), slot + 1, 0)
        lane3 = lax.broadcasted_iota(jnp.int32, (CSLOT, BLK), 1)
        mine_c, other_c = idx_ref[...] + 1, idx_c[...] + 1
        for i in (0, 1):
            tab_v[i] = jnp.where(
                lane3 < BLK // 2, column(mine_c[4 + i : 5 + i], CSLOT), column(other_c[4 + i : 5 + i], CSLOT)
            )

        def one_slot(s, carry):
            out_row, out_col = tab_v[0, pl.ds(s, 1)], tab_v[1, pl.ds(s, 1)]
            found = jnp.max(jnp.where(row_col == out_row, weight, 0), axis=0, keepdims=True)
            place = jnp.clip(2 * found - 2 + second, 0, ZERO)
            tab_v[2, pl.ds(s, 1)] = jnp.where((found > 0) & (out_col == b_to), place, ZERO)
            return carry

        lax.fori_loop(0, CSLOT, one_slot, 0)
        for copy in (tab_copy, low_copy):
            copy.start()

    tab_copy = pltpu.make_async_copy(tab_v.at[2], tab_s, s_tab.at[0])
    low_copy = pltpu.make_async_copy(low_v, low_s, s_tab.at[1])

    def spread(o, zz, slot):
        return remote(bbuf.at[o, zz], bbuf.at[o, zz], s_bx.at[slot], r_b.at[o, zz], twin)

    def split_b(o, zz):
        def one(i, carry):
            value = bbuf[o, zz, i]
            high = value.astype(jnp.bfloat16)
            bhi[o, zz, i] = high
            blo[o, zz, i] = (value - high.astype(jnp.float32)).astype(jnp.bfloat16)
            return carry

        lax.fori_loop(0, BSLOT, one, 0)

    def b_slot(i):
        return q * NY + (y + i) % NY

    def b_here(o, i):
        landed(bbuf.at[o, b_slot(i)], r_b.at[o, b_slot(i)])

    def b_next(way):
        zz = b_slot(0)
        return remote(bbuf.at[1, zz], bbuf.at[1, zz], s_bn.at[way], r_b.at[1, zz], (up, down)[way])

    def b_pass(o):
        zz = b_slot(3 if o == 0 else 1)
        return remote(bbuf.at[o, zz], bbuf.at[o, zz], s_bf.at[o], r_b.at[o, zz], (up, down)[o])

    def b_done(o, i):
        spread(o, b_slot(i), i * 2 + o).start()
        split_b(o, b_slot(i))

    def a_step(dist, j):
        from_left(dist, j)
        a_right(dist, j).start()
        from_right(dist, j)
        a_left(dist, j).start()

    a_step(1, 0)
    b_here(0, 0)
    b_done(0, 0)
    a_step(1, 1)
    b_here(1, 0)
    b_next(0).start()
    b_next(1).start()
    b_done(1, 0)
    a_step(1, 2)
    b_here(0, 3)
    b_pass(0).start()
    b_here(0, 1)
    b_done(0, 3)
    b_done(0, 1)
    a_step(1, 3)
    tables()
    b_here(1, 1)
    b_pass(1).start()
    b_here(1, 3)
    b_done(1, 1)
    b_done(1, 3)
    a_step(2, 0)
    b_here(0, 2)
    b_done(0, 2)
    a_step(2, 1)
    b_here(1, 2)
    b_done(1, 2)
    for j in (2, 3):
        from_left(2, j)
        from_right(2, j)
    a_step(3, 0)
    for j in (2, 3):
        a_right(2, j).start()
        a_left(2, j).start()

    def take_b(i, carry):
        o, zz = i // NY, (1 - q) * NY + i % NY
        landed(bbuf.at[o, zz], r_b.at[o, zz])
        split_b(o, zz)
        return carry

    lax.fori_loop(0, 2 * NY, take_b, 0)
    for p in range(PARTS):
        local_a(p).wait()
    tab_copy.wait()
    low_copy.wait()

    def multiply(zz, first, count):
        rows = count * PROW

        def one(a):
            value = abuf[zz, first : first + count, a].reshape(rows, BLK)
            high = value.astype(jnp.bfloat16)
            low = (value - high.astype(jnp.float32)).astype(jnp.bfloat16)
            both = jnp.concatenate([high, low], axis=0)
            for o in (0, 1):
                b0 = low_s[2 * o, zz * LANE_A + a]
                b1 = low_s[2 * o + 1, zz * LANE_A + a]
                wide = jnp.concatenate([bhi[o, zz, b0], bhi[o, zz, b1]], axis=1)
                fine = jnp.concatenate([blo[o, zz, b0], blo[o, zz, b1]], axis=1)
                big = jnp.dot(both, wide, preferred_element_type=jnp.float32)
                small = jnp.dot(high, fine, preferred_element_type=jnp.float32)
                total = big[:rows] + (big[rows:] + small)
                for v in range(rows // SROW):
                    span = first * PROW // SROW + v
                    prods[span, o, 2 * a] = total[v * SROW : (v + 1) * SROW, :BLK]
                    prods[span, o, 2 * a + 1] = total[v * SROW : (v + 1) * SROW, BLK:]

        def some(i, carry):
            for j in range(UNROLL):
                one(i * UNROLL + j)
            return carry

        lax.fori_loop(0, ASLOT // UNROLL, some, 0)

    def gather(zz, o, spans, begin, end):
        base = o * (BLK // 2) + zz * BSLOT

        def some(i, carry):
            for j in (0, 1):
                s = i * 2 + j
                at = [tab_s[s, base + b] for b in range(BSLOT)]
                for v in spans:
                    terms = [prods[v, o, p] for p in at]
                    while len(terms) > 1:
                        terms = [x + w for x, w in zip(terms[::2], terms[1::2])]
                    acc[v, o, s] += terms[0]
            return carry

        lax.fori_loop(begin // 2, end // 2, some, 0)

    def near(k, carry):
        step = (k + 1) // 2
        zz = (z + NZ + jnp.where(k % 2 == 1, step, -step)) % NZ
        multiply(zz, 0, PARTS)
        for o in (0, 1):
            gather(zz, o, range(SPANS), 0, CSLOT)
        return carry

    lax.fori_loop(0, 5, near, 0)

    def c_piece(v, o, j):
        return acc.at[v, o, pl.ds(j * CSZ, CSZ)]

    def c_landing(v, j):
        return crecv.at[v, pl.ds(j * CSZ, CSZ)]

    def send_c(v, j):
        return remote(c_piece(v, 1, j), c_landing(v, j), s_c.at[v, j], r_c.at[v, j], partner)

    def out_piece(v, j, which):
        return o_ref.at[pl.ds(j * CSZ, CSZ), 0, pl.ds(which * ROWS + v * SROW, SROW), :]

    def send_m(v, j):
        return remote(c_piece(v, 0, j), out_piece(v, j, half), s_m.at[v, j], r_m.at[v, j], mate)

    def store_o(v, j):
        return pltpu.make_async_copy(c_piece(v, 0, j), out_piece(v, j, half), s_o.at[v, j])

    far = ((z + 3) % NZ, (z + NZ - 3) % NZ)
    last = (z + 4) % NZ
    for v in range(SPANS):
        if v == 0:
            from_left(3, 2)
            a_right(3, 2).start()
            from_right(3, 2)
            a_left(3, 2).start()
        from_left(3, 2 * v + 1)
        from_right(3, 2 * v + 1)
        for zz in far:
            multiply(zz, 2 * v, 2)
            for o in (0, 1):
                gather(zz, o, (v,), 0, CSLOT)
        from_left(4, 2 * v)
        from_right(4, 2 * v)
        multiply(last, 2 * v, 2)
        for j in range(CCH):
            gather(last, 1, (v,), j * CSZ, (j + 1) * CSZ)
            send_c(v, j).start()
        gather(last, 0, (v,), 0, CSLOT)
    for v in range(SPANS):
        for j in range(CCH):
            landed(c_landing(v, j), r_c.at[v, j])

            def add(s, carry):
                acc[v, 0, s] += crecv[v, s]
                return carry

            lax.fori_loop(j * CSZ, (j + 1) * CSZ, add, 0)
            send_m(v, j).start()
            store_o(v, j).start()

    for v in range(SPANS):
        for j in range(CCH):
            landed(out_piece(v, j, 1 - half), r_m.at[v, j])
            store_o(v, j).wait()
            send_m(v, j).wait_send()
            send_c(v, j).wait_send()

    def end_ia(i, carry):
        send_ia(i).wait_send()
        return carry

    def end_ib(i, carry):
        pl.when(other_ib(i))(lambda: send_ib(i).wait_send())
        return carry

    lax.fori_loop(1, NZ, end_ia, 0)
    lax.fori_loop(0, 2 * NY, end_ib, 0)
    send_ic.wait_send()

    @pl.when(own)
    def _():
        for s in (0, 1):
            pl.when(q != s)(lambda: send_bd(0, s).wait_send())
            send_bd(1, s).wait_send()
            send_bd(3, s).wait_send()

    @pl.when(jnp.logical_not(own))
    def _():
        send_bp(0).wait_send()
        send_bp(1).wait_send()

    for o in (0, 1):
        b_next(o).wait_send()
        b_pass(o).wait_send()
        for i in range(NY):
            spread(o, b_slot(i), i * 2 + o).wait_send()

    def end_a(j, carry):
        for dist in range(3):
            a_right(dist, j).wait_send()
            a_left(dist, j).wait_send()

        @pl.when(j % 2 == 0)
        def _():
            a_right(3, j).wait_send()
            a_left(3, j).wait_send()

        return carry

    lax.fori_loop(0, PARTS, end_a, 0)


UNROLL = 4


def index_rows(a_index, b_index, c_index):
    def wide(part):
        return jnp.pad(part, ((0, 0), (0, BLK - part.shape[1])), constant_values=-1)

    b_rows = jnp.pad(b_index[..., 0], ((0, 0), (0, 0), (0, BLK // 4 - BSLOT)), constant_values=-1)
    rows = [a_index[:, :, 0], b_rows.reshape(2, BLK // 2), c_index[:, :, 0], jnp.full((2, BLK), -1, jnp.int32)]
    return jnp.concatenate([wide(part) for part in rows], axis=0)


def local(a_blocks, a_index, b_blocks, b_index, c_index):
    dma = pltpu.SemaphoreType.DMA
    f32, bf16, i32 = jnp.float32, jnp.bfloat16, jnp.int32
    anywhere = pl.BlockSpec(memory_space=pl.ANY)
    return pl.pallas_call(
        kernel,
        out_shape=jax.ShapeDtypeStruct((CSLOT, 1, BLK, BLK), f32),
        in_specs=[pl.BlockSpec(memory_space=pltpu.VMEM), anywhere, anywhere],
        out_specs=anywhere,
        scratch_shapes=[
            pltpu.VMEM((NZ, 8, BLK), i32),
            pltpu.VMEM((2 * NY, 8, BLK), i32),
            pltpu.VMEM((8, BLK), i32),
            pltpu.VMEM((3, CSLOT, BLK), i32),
            pltpu.VMEM((8, 2 * BLK), i32),
            pltpu.SMEM((CSLOT, BLK), i32),
            pltpu.SMEM((8, 2 * BLK), i32),
            pltpu.VMEM((NZ, PARTS, ASLOT, PROW, BLK), f32),
            pltpu.VMEM((2, NZ, BSLOT, BLK, BLK), f32),
            pltpu.VMEM((2, NZ, BSLOT, BLK, BLK), bf16),
            pltpu.VMEM((2, NZ, BSLOT, BLK, BLK), bf16),
            pltpu.VMEM((SPANS, 2, ZERO + 1, SROW, BLK), f32),
            pltpu.VMEM((SPANS, 2, CSLOT, SROW, BLK), f32),
            pltpu.VMEM((SPANS, CSLOT, SROW, BLK), f32),
            dma((NZ,)), dma((NZ,)), dma((2 * NY,)), dma((2 * NY,)), dma, dma, dma((2,)),
            dma((4, PARTS)), dma((4, PARTS)), dma((NZ, PARTS)), dma((PARTS,)),
            dma((NY, 2)), dma((2,)), dma((2,)), dma((2 * NY,)), dma((2, NZ)),
            dma((SPANS, CCH)), dma((SPANS, CCH)), dma((SPANS, CCH)), dma((SPANS, CCH)), dma((SPANS, CCH)),
        ],
        compiler_params=pltpu.CompilerParams(
            collective_id=0, has_side_effects=True, vmem_limit_bytes=56 * 1024 * 1024
        ),
        cost_estimate=pl.CostEstimate(flops=10**10, bytes_accessed=10**7, transcendentals=0),
    )(index_rows(a_index, b_index, c_index), a_blocks, b_blocks)


def solution(mesh):
    in_specs = (
        P("row", "col", None, None),
        P(None, "row", "col"),
        P(None, "row", "col", None, None),
        P(None, None, "row", "col"),
        P(None, "row", "col"),
    )
    out_specs = P("row", "col", None, None)
    return jax.shard_map(local, mesh=mesh, in_specs=in_specs, out_specs=out_specs, check_vma=False)
```

```python
import functools

import jax
import jax.numpy as jnp
from jax import lax
from jax.experimental import pallas as pl
from jax.experimental.pallas import tpu as pltpu
from jax.sharding import PartitionSpec as P

MESH = pl.DeviceIdType.MESH
NZ, NY = 8, 4
ASLOT, BSLOT, CSLOT, BLK = 24, 8, 32, 128
ROWS = BLK // 2
PARTS, PROW = 4, ROWS // 4
SPANS, SROW = 2, ROWS // 2
CCH, CSZ = 4, CSLOT // 4
LANE_A = 32
ZERO = 2 * ASLOT


def kernel(
    idx_ref, a_ref, b_ref, o_ref,
    idx_a, idx_b, idx_c, tab_v, low_v, tab_s, low_s,
    abuf, bbuf, bhi, blo, prods, acc, crecv,
    s_ia, r_ia, s_ib, r_ib, s_ic, r_ic, s_tab,
    s_al, s_ar, r_a, s_loc, s_bd, s_bn, s_bf, s_bx, r_b, s_c, r_c, s_o, s_m, r_m,
):
    r = lax.axis_index("row")
    c = lax.axis_index("col")
    d = lax.axis_index("depth")
    y, q = r // 2, r % 2
    z, h = c // 2, c % 2
    half = (h + d) % 2
    own = q == h
    role = (q + h) % 2
    b_col = z * 2 + q
    b_depth = (d + h + q) % 2
    partner = (r, z * 2 + 1 - h, 1 - d)
    mate = (r, c, 1 - d)
    twin = (y * 2 + 1 - q, c, d)
    up, down = (((y + 1) % NY) * 2 + q, c, d), (((y + 3) % NY) * 2 + q, c, d)
    right, left = (r, ((z + 1) % NZ) * 2 + h, d), (r, ((z + 7) % NZ) * 2 + h, d)

    def remote(src, dst, send, recv, device):
        return pltpu.make_async_remote_copy(
            src_ref=src, dst_ref=dst, send_sem=send, recv_sem=recv, device_id=device, device_id_type=MESH
        )

    def landed(ref, sem):
        pltpu.make_async_copy(ref, ref, sem).wait()

    barrier = pltpu.get_barrier_semaphore()

    def greet(device):
        pl.semaphore_signal(barrier, inc=1, device_id=device, device_id_type=MESH)

    def greet_z(i, carry):
        greet((r, ((z + i) % NZ) * 2 + h, d))
        return carry

    lax.fori_loop(1, NZ, greet_z, 0)

    def greet_b(i, carry):
        yy = (y + i) % NY
        greet((yy * 2 + h, z * 2 + 1 - h, 1 - d))

        @pl.when(jnp.logical_not(own & (i == 0)))
        def _():
            greet((yy * 2 + h, c, d))

        return carry

    lax.fori_loop(0, NY, greet_b, 0)
    for device in (partner, mate, twin, up, down):
        greet(device)
    pl.semaphore_wait(barrier, NZ - 1 + 2 * NY + 5 - own.astype(jnp.int32))

    def send_bd(i, s):
        yy = (y + i) % NY
        return remote(b_ref.at[s, :, 0], bbuf.at[0, s * NY + y], s_bd.at[i, s], r_b.at[0, s * NY + y], (yy * 2 + s, c, d))

    def send_bp(s):
        return remote(
            b_ref.at[s, :, 0], bbuf.at[1, s * NY + y], s_bd.at[0, s], r_b.at[1, s * NY + y],
            (y * 2 + s, z * 2 + 1 - h, 1 - d),
        )

    local_b = pltpu.make_async_copy(b_ref.at[q, :, 0], bbuf.at[0, q * NY + y], r_b.at[0, q * NY + y])

    @pl.when(own)
    def _():
        for s in (0, 1):
            pl.when(q != s)(lambda: send_bd(0, s).start())
            send_bd(1, s).start()
            send_bd(3, s).start()
        local_b.start()

    @pl.when(jnp.logical_not(own))
    def _():
        send_bp(0).start()
        send_bp(1).start()

    def own_part(p):
        return a_ref.at[:, 0, pl.ds(half * ROWS + p * PROW, PROW), :]

    def part(zz, p):
        return abuf.at[zz, p]

    def turn(j):
        return j + 1 - 2 * (j % 2)

    def a_right(dist, j):
        zz = (z + NZ - dist) % NZ
        return remote(part(zz, j), part(zz, j), s_ar.at[dist, j], r_a.at[zz, j], right)

    def a_left(dist, j):
        zz, p = (z + dist) % NZ, turn(j)
        return remote(part(zz, p), part(zz, p), s_al.at[dist, j], r_a.at[zz, p], left)

    def from_left(dist, j):
        zz = (z + NZ - dist) % NZ
        landed(part(zz, j), r_a.at[zz, j])

    def from_right(dist, j):
        zz, p = (z + dist) % NZ, turn(j)
        landed(part(zz, p), r_a.at[zz, p])

    def local_a(p):
        return pltpu.make_async_copy(own_part(p), part(z, p), s_loc.at[p])

    def start_a(j, carry):
        p = turn(j)
        remote(own_part(j), part(z, j), s_ar.at[0, j], r_a.at[z, j], right).start()
        remote(own_part(p), part(z, p), s_al.at[0, j], r_a.at[z, p], left).start()
        local_a(j).start()
        return carry

    lax.fori_loop(0, PARTS, start_a, 0)

    def send_ia(i):
        return remote(idx_ref, idx_a.at[z], s_ia.at[i], r_ia.at[z], (r, ((z + i) % NZ) * 2 + h, d))

    def send_ib(i):
        yy, core = (y + i // 2) % NY, i % 2
        at = role * NY + y
        return remote(idx_ref, idx_b.at[at], s_ib.at[i], r_ib.at[at], (yy * 2 + core, b_col, b_depth))

    def other_ib(i):
        return jnp.logical_not(own & (i // 2 == 0) & (i % 2 == q))

    send_ic = remote(idx_ref, idx_c, s_ic, r_ic, partner)

    def start_ia(i, carry):
        send_ia(i).start()
        return carry

    def start_ib(i, carry):
        pl.when(other_ib(i))(lambda: send_ib(i).start())
        return carry

    lax.fori_loop(1, NZ, start_ia, 0)
    lax.fori_loop(0, 2 * NY, start_ib, 0)
    send_ic.start()
    idx_a[z] = idx_ref[...]

    @pl.when(own)
    def _():
        idx_b[y] = idx_ref[...]

    acc[...] = jnp.zeros_like(acc)
    for v in range(SPANS):
        for o in (0, 1):
            prods[v, o, ZERO] = jnp.zeros((SROW, BLK), jnp.float32)

    def tables():
        def wait_ia(i, carry):
            zz = (z + i) % NZ
            landed(idx_a.at[zz], r_ia.at[zz])
            return carry

        lax.fori_loop(1, NZ, wait_ia, 0)

        def wait_ib(i, carry):
            yy = (y + i) % NY
            landed(idx_b.at[NY + yy], r_ib.at[NY + yy])
            pl.when(jnp.logical_not(own & (i == 0)))(lambda: landed(idx_b.at[yy], r_ib.at[yy]))
            return carry

        lax.fori_loop(0, NY, wait_ib, 0)
        landed(idx_c, r_ic)

        a_sets = []
        for g in (0, 1):
            rolled = [pltpu.roll(idx_a[g * 4 + i] + 1, i * LANE_A, 1) if i else idx_a[g * 4] + 1 for i in range(4)]
            a_sets.append(rolled[0] + rolled[1] + (rolled[2] + rolled[3]))
        rolled = [pltpu.roll(idx_b[i] + 1, (i // NY) * (BLK // 2) + (i % NY) * BSLOT, 1) if i else idx_b[0] + 1 for i in range(2 * NY)]
        while len(rolled) > 1:
            rolled = [x + w for x, w in zip(rolled[::2], rolled[1::2])]
        b_key, b_to = rolled[0][2:3], rolled[0][3:4]
        a_in = jnp.concatenate([a_sets[0][1:2], a_sets[1][1:2]], axis=1)

        def column(row, count):
            wide = jnp.broadcast_to(row, (count, BLK))
            at = lax.broadcasted_iota(jnp.int32, (count, BLK), 0)
            lane = lax.broadcasted_iota(jnp.int32, (count, BLK), 1)
            return jnp.sum(jnp.where(at == lane, wide, 0), axis=1, keepdims=True)

        key_col = column(b_key, BLK)
        at = lax.broadcasted_iota(jnp.int32, (BLK, 2 * BLK), 0)
        match = (key_col == a_in) & (a_in > 0)
        low_v[...] = jnp.zeros_like(low_v)
        for o in (0, 1):
            mine = match & (at // (BLK // 2) == o)
            first = jnp.min(jnp.where(mine, at % BSLOT, BSLOT), axis=0, keepdims=True)
            last = jnp.max(jnp.where(mine, at % BSLOT, 0), axis=0, keepdims=True)
            low_v[2 * o : 2 * o + 1] = jnp.where(first == BSLOT, 0, first)
            low_v[2 * o + 1 : 2 * o + 2] = last
        at2 = at[:, :BLK]
        lane2 = lax.broadcasted_iota(jnp.int32, (BLK, BLK), 1)
        earlier = (key_col == b_key) & (at2 < lane2) & (at2 // (BLK // 2) == lane2 // (BLK // 2))
        second = jnp.max(jnp.where(earlier, 1, 0), axis=0, keepdims=True)
        row_col = jnp.concatenate([column(a_sets[g][0:1], BLK) for g in (0, 1)], axis=0)
        in_col = jnp.concatenate([column(a_sets[g][1:2], BLK) for g in (0, 1)], axis=0)
        slot = lax.broadcasted_iota(jnp.int32, (2 * BLK, BLK), 0) % LANE_A
        weight = jnp.where((in_col == b_key) & (in_col > 0), slot + 1, 0)
        lane3 = lax.broadcasted_iota(jnp.int32, (CSLOT, BLK), 1)
        mine_c, other_c = idx_ref[...] + 1, idx_c[...] + 1
        for i in (0, 1):
            tab_v[i] = jnp.where(
                lane3 < BLK // 2, column(mine_c[4 + i : 5 + i], CSLOT), column(other_c[4 + i : 5 + i], CSLOT)
            )

        def one_slot(s, carry):
            out_row, out_col = tab_v[0, pl.ds(s, 1)], tab_v[1, pl.ds(s, 1)]
            found = jnp.max(jnp.where(row_col == out_row, weight, 0), axis=0, keepdims=True)
            place = jnp.clip(2 * found - 2 + second, 0, ZERO)
            tab_v[2, pl.ds(s, 1)] = jnp.where((found > 0) & (out_col == b_to), place, ZERO)
            return carry

        lax.fori_loop(0, CSLOT, one_slot, 0)
        for copy in (tab_copy, low_copy):
            copy.start()

    tab_copy = pltpu.make_async_copy(tab_v.at[2], tab_s, s_tab.at[0])
    low_copy = pltpu.make_async_copy(low_v, low_s, s_tab.at[1])

    def spread(o, zz, slot):
        return remote(bbuf.at[o, zz], bbuf.at[o, zz], s_bx.at[slot], r_b.at[o, zz], twin)

    def split_b(o, zz):
        def one(i, carry):
            value = bbuf[o, zz, i]
            high = value.astype(jnp.bfloat16)
            bhi[o, zz, i] = high
            blo[o, zz, i] = (value - high.astype(jnp.float32)).astype(jnp.bfloat16)
            return carry

        lax.fori_loop(0, BSLOT, one, 0)

    def b_slot(i):
        return q * NY + (y + i) % NY

    def b_here(o, i):
        landed(bbuf.at[o, b_slot(i)], r_b.at[o, b_slot(i)])

    def b_next(way):
        zz = b_slot(0)
        return remote(bbuf.at[1, zz], bbuf.at[1, zz], s_bn.at[way], r_b.at[1, zz], (up, down)[way])

    def b_pass(o):
        zz = b_slot(3 if o == 0 else 1)
        return remote(bbuf.at[o, zz], bbuf.at[o, zz], s_bf.at[o], r_b.at[o, zz], (up, down)[o])

    def b_done(o, i):
        spread(o, b_slot(i), i * 2 + o).start()
        split_b(o, b_slot(i))

    def a_step(dist, j):
        from_left(dist, j)
        a_right(dist, j).start()
        from_right(dist, j)
        a_left(dist, j).start()

    a_step(1, 0)
    b_here(0, 0)
    b_done(0, 0)
    a_step(1, 1)
    b_here(1, 0)
    b_next(0).start()
    b_next(1).start()
    b_done(1, 0)
    a_step(1, 2)
    b_here(0, 3)
    b_pass(0).start()
    b_here(0, 1)
    b_done(0, 3)
    b_done(0, 1)
    a_step(1, 3)
    tables()
    b_here(1, 1)
    b_pass(1).start()
    b_here(1, 3)
    b_done(1, 1)
    b_done(1, 3)
    a_step(2, 0)
    b_here(0, 2)
    b_done(0, 2)
    a_step(2, 1)
    b_here(1, 2)
    b_done(1, 2)
    for j in (2, 3):
        from_left(2, j)
        from_right(2, j)
    a_step(3, 0)
    for j in (2, 3):
        a_right(2, j).start()
        a_left(2, j).start()

    def take_b(i, carry):
        o, zz = i // NY, (1 - q) * NY + i % NY
        landed(bbuf.at[o, zz], r_b.at[o, zz])
        split_b(o, zz)
        return carry

    lax.fori_loop(0, 2 * NY, take_b, 0)
    for p in range(PARTS):
        local_a(p).wait()
    tab_copy.wait()
    low_copy.wait()

    def multiply(zz, first, count, outs):
        rows = count * PROW
        unroll = UNROLL if len(outs) == 2 else UNROLL + UNROLL // 2

        def one(a):
            value = abuf[zz, first : first + count, a].reshape(rows, BLK)
            high = value.astype(jnp.bfloat16)
            low = (value - high.astype(jnp.float32)).astype(jnp.bfloat16)
            twice = [jnp.concatenate([part, part], axis=1) for part in (high, low)]
            both = jnp.concatenate(twice, axis=0)
            for o in outs:
                b0 = low_s[2 * o, zz * LANE_A + a]
                b1 = low_s[2 * o + 1, zz * LANE_A + a]
                wide = jnp.concatenate([bhi[o, zz, b0], bhi[o, zz, b1]], axis=1)
                fine = jnp.concatenate([blo[o, zz, b0], blo[o, zz, b1]], axis=1)
                big = jnp.dot(both, jnp.concatenate([wide, fine], axis=0), preferred_element_type=jnp.float32)
                total = big[:rows] + big[rows:]
                for v in range(rows // SROW):
                    span = first * PROW // SROW + v
                    prods[span, o, 2 * a] = total[v * SROW : (v + 1) * SROW, :BLK]
                    prods[span, o, 2 * a + 1] = total[v * SROW : (v + 1) * SROW, BLK:]

        def some(i, carry):
            for j in range(unroll):
                one(i * unroll + j)
            return carry

        lax.fori_loop(0, ASLOT // unroll, some, 0)

    def gather(zz, o, spans, begin, end):
        base = o * (BLK // 2) + zz * BSLOT

        def some(i, carry):
            for j in range(CSZ):
                s = i * CSZ + j
                at = [tab_s[s, base + b] for b in range(BSLOT)]
                for v in spans:
                    terms = [prods[v, o, p] for p in at]
                    while len(terms) > 1:
                        terms = [x + w for x, w in zip(terms[::2], terms[1::2])]
                    acc[v, o, s] += terms[0]
            return carry

        lax.fori_loop(begin // CSZ, end // CSZ, some, 0)

    def near(o):
        def one(k, carry):
            step = (k + 1) // 2
            zz = (z + NZ + jnp.where(k % 2 == 1, step, -step)) % NZ
            multiply(zz, 0, PARTS, (o,))
            gather(zz, o, range(SPANS), 0, CSLOT)
            return carry

        lax.fori_loop(0, 5, one, 0)

    near(1)
    from_left(3, 2)
    a_right(3, 2).start()
    from_right(3, 2)
    a_left(3, 2).start()
    near(0)

    def c_piece(v, o, j):
        return acc.at[v, o, pl.ds(j * CSZ, CSZ)]

    def c_landing(v, j):
        return crecv.at[v, pl.ds(j * CSZ, CSZ)]

    def send_c(v, j):
        return remote(c_piece(v, 1, j), c_landing(v, j), s_c.at[v, j], r_c.at[v, j], partner)

    def out_piece(v, j, which):
        return o_ref.at[pl.ds(j * CSZ, CSZ), 0, pl.ds(which * ROWS + v * SROW, SROW), :]

    def send_m(v, j):
        return remote(c_piece(v, 0, j), out_piece(v, j, half), s_m.at[v, j], r_m.at[v, j], mate)

    def store_o(v, j):
        return pltpu.make_async_copy(c_piece(v, 0, j), out_piece(v, j, half), s_o.at[v, j])

    def far(v, o):
        def one(i, carry):
            zz = (z + 3 + 2 * i) % NZ
            multiply(zz, 2 * v, 2, (o,))
            gather(zz, o, (v,), 0, CSLOT)
            return carry

        lax.fori_loop(0, 2, one, 0)

    def finish(v, j):
        landed(c_landing(v, j), r_c.at[v, j])

        def add(s, carry):
            acc[v, 0, s] += crecv[v, s]
            return carry

        lax.fori_loop(j * CSZ, (j + 1) * CSZ, add, 0)
        send_m(v, j).start()
        store_o(v, j).start()

    last = (z + 4) % NZ
    for v in range(SPANS):
        from_left(3, 2 * v + 1)
        from_right(3, 2 * v + 1)
        far(v, 1)
        from_left(4, 2 * v)
        from_right(4, 2 * v)
        multiply(last, 2 * v, 2, (1,))

        def give(j, carry):
            gather(last, 1, (v,), j * CSZ, (j + 1) * CSZ)
            send_c(v, j).start()
            return carry

        lax.fori_loop(0, CCH, give, 0)
        if v:
            finish(0, 2)
            finish(0, 3)
        far(v, 0)
        multiply(last, 2 * v, 2, (0,))
        gather(last, 0, (v,), 0, CSLOT)
        if v == 0:
            finish(0, 0)
            finish(0, 1)
    for j in range(CCH):
        finish(1, j)

    for v in range(SPANS):
        for j in range(CCH):
            landed(out_piece(v, j, 1 - half), r_m.at[v, j])
            store_o(v, j).wait()
            send_m(v, j).wait_send()
            send_c(v, j).wait_send()

    def end_ia(i, carry):
        send_ia(i).wait_send()
        return carry

    def end_ib(i, carry):
        pl.when(other_ib(i))(lambda: send_ib(i).wait_send())
        return carry

    lax.fori_loop(1, NZ, end_ia, 0)
    lax.fori_loop(0, 2 * NY, end_ib, 0)
    send_ic.wait_send()

    @pl.when(own)
    def _():
        for s in (0, 1):
            pl.when(q != s)(lambda: send_bd(0, s).wait_send())
            send_bd(1, s).wait_send()
            send_bd(3, s).wait_send()

    @pl.when(jnp.logical_not(own))
    def _():
        send_bp(0).wait_send()
        send_bp(1).wait_send()

    for o in (0, 1):
        b_next(o).wait_send()
        b_pass(o).wait_send()
        for i in range(NY):
            spread(o, b_slot(i), i * 2 + o).wait_send()

    def end_a(j, carry):
        for dist in range(3):
            a_right(dist, j).wait_send()
            a_left(dist, j).wait_send()

        @pl.when(j % 2 == 0)
        def _():
            a_right(3, j).wait_send()
            a_left(3, j).wait_send()

        return carry

    lax.fori_loop(0, PARTS, end_a, 0)


UNROLL = 8


def index_rows(a_index, b_index, c_index):
    def wide(part):
        return jnp.pad(part, ((0, 0), (0, BLK - part.shape[1])), constant_values=-1)

    b_rows = jnp.pad(b_index[..., 0], ((0, 0), (0, 0), (0, BLK // 4 - BSLOT)), constant_values=-1)
    rows = [a_index[:, :, 0], b_rows.reshape(2, BLK // 2), c_index[:, :, 0], jnp.full((2, BLK), -1, jnp.int32)]
    return jnp.concatenate([wide(part) for part in rows], axis=0)


def local(a_blocks, a_index, b_blocks, b_index, c_index):
    dma = pltpu.SemaphoreType.DMA
    f32, bf16, i32 = jnp.float32, jnp.bfloat16, jnp.int32
    anywhere = pl.BlockSpec(memory_space=pl.ANY)
    return pl.pallas_call(
        kernel,
        out_shape=jax.ShapeDtypeStruct((CSLOT, 1, BLK, BLK), f32),
        in_specs=[pl.BlockSpec(memory_space=pltpu.VMEM), anywhere, anywhere],
        out_specs=anywhere,
        scratch_shapes=[
            pltpu.VMEM((NZ, 8, BLK), i32),
            pltpu.VMEM((2 * NY, 8, BLK), i32),
            pltpu.VMEM((8, BLK), i32),
            pltpu.VMEM((3, CSLOT, BLK), i32),
            pltpu.VMEM((8, 2 * BLK), i32),
            pltpu.SMEM((CSLOT, BLK), i32),
            pltpu.SMEM((8, 2 * BLK), i32),
            pltpu.VMEM((NZ, PARTS, ASLOT, PROW, BLK), f32),
            pltpu.VMEM((2, NZ, BSLOT, BLK, BLK), f32),
            pltpu.VMEM((2, NZ, BSLOT, BLK, BLK), bf16),
            pltpu.VMEM((2, NZ, BSLOT, BLK, BLK), bf16),
            pltpu.VMEM((SPANS, 2, ZERO + 1, SROW, BLK), f32),
            pltpu.VMEM((SPANS, 2, CSLOT, SROW, BLK), f32),
            pltpu.VMEM((SPANS, CSLOT, SROW, BLK), f32),
            dma((NZ,)), dma((NZ,)), dma((2 * NY,)), dma((2 * NY,)), dma, dma, dma((2,)),
            dma((4, PARTS)), dma((4, PARTS)), dma((NZ, PARTS)), dma((PARTS,)),
            dma((NY, 2)), dma((2,)), dma((2,)), dma((2 * NY,)), dma((2, NZ)),
            dma((SPANS, CCH)), dma((SPANS, CCH)), dma((SPANS, CCH)), dma((SPANS, CCH)), dma((SPANS, CCH)),
        ],
        compiler_params=pltpu.CompilerParams(
            collective_id=0, has_side_effects=True, vmem_limit_bytes=56 * 1024 * 1024
        ),
        cost_estimate=pl.CostEstimate(flops=10**10, bytes_accessed=10**7, transcendentals=0),
    )(index_rows(a_index, b_index, c_index), a_blocks, b_blocks)


def solution(mesh):
    in_specs = (
        P("row", "col", None, None),
        P(None, "row", "col"),
        P(None, "row", "col", None, None),
        P(None, None, "row", "col"),
        P(None, "row", "col"),
    )
    out_specs = P("row", "col", None, None)
    return jax.shard_map(local, mesh=mesh, in_specs=in_specs, out_specs=out_specs, check_vma=False)
```

```python
import functools

import jax
import jax.numpy as jnp
from jax import lax
from jax.experimental import pallas as pl
from jax.experimental.pallas import tpu as pltpu
from jax.sharding import PartitionSpec as P

MESH = pl.DeviceIdType.MESH
NZ, NY = 8, 4
ASLOT, BSLOT, CSLOT, BLK = 24, 8, 32, 128
ROWS = BLK // 2
PARTS, PROW = 4, ROWS // 4
SPANS, SROW = 2, ROWS // 2
CCH, CSZ = 4, CSLOT // 4
LANE_A = 32
ZERO = 2 * ASLOT


def kernel(
    idx_ref, a_ref, b_ref, o_ref,
    idx_a, idx_b, idx_c, tab_v, low_v, tab_s, low_s,
    abuf, bbuf, bhi, blo, prods, acc, crecv,
    s_ia, r_ia, s_ib, r_ib, s_ic, r_ic, s_tab,
    s_al, s_ar, r_a, s_loc, s_bd, s_bn, s_bf, s_bx, r_b, s_c, r_c, s_o, s_m, r_m,
):
    r = lax.axis_index("row")
    c = lax.axis_index("col")
    d = lax.axis_index("depth")
    y, q = r // 2, r % 2
    z, h = c // 2, c % 2
    half = (h + d) % 2
    own = q == h
    role = (q + h) % 2
    b_col = z * 2 + q
    b_depth = (d + h + q) % 2
    partner = (r, z * 2 + 1 - h, 1 - d)
    mate = (r, c, 1 - d)
    twin = (y * 2 + 1 - q, c, d)
    up, down = (((y + 1) % NY) * 2 + q, c, d), (((y + 3) % NY) * 2 + q, c, d)
    right, left = (r, ((z + 1) % NZ) * 2 + h, d), (r, ((z + 7) % NZ) * 2 + h, d)

    def remote(src, dst, send, recv, device):
        return pltpu.make_async_remote_copy(
            src_ref=src, dst_ref=dst, send_sem=send, recv_sem=recv, device_id=device, device_id_type=MESH
        )

    def landed(ref, sem):
        pltpu.make_async_copy(ref, ref, sem).wait()

    barrier = pltpu.get_barrier_semaphore()

    def greet(device):
        pl.semaphore_signal(barrier, inc=1, device_id=device, device_id_type=MESH)

    def greet_z(i, carry):
        greet((r, ((z + i) % NZ) * 2 + h, d))
        return carry

    lax.fori_loop(1, NZ, greet_z, 0)

    def greet_b(i, carry):
        yy = (y + i) % NY
        greet((yy * 2 + h, z * 2 + 1 - h, 1 - d))

        @pl.when(jnp.logical_not(own & (i == 0)))
        def _():
            greet((yy * 2 + h, c, d))

        return carry

    lax.fori_loop(0, NY, greet_b, 0)
    for device in (partner, mate, twin, up, down):
        greet(device)
    pl.semaphore_wait(barrier, NZ - 1 + 2 * NY + 5 - own.astype(jnp.int32))

    def send_bd(i, s):
        yy = (y + i) % NY
        return remote(b_ref.at[s, :, 0], bbuf.at[0, s * NY + y], s_bd.at[i, s], r_b.at[0, s * NY + y], (yy * 2 + s, c, d))

    def send_bp(s):
        return remote(
            b_ref.at[s, :, 0], bbuf.at[1, s * NY + y], s_bd.at[0, s], r_b.at[1, s * NY + y],
            (y * 2 + s, z * 2 + 1 - h, 1 - d),
        )

    local_b = pltpu.make_async_copy(b_ref.at[q, :, 0], bbuf.at[0, q * NY + y], r_b.at[0, q * NY + y])

    @pl.when(own)
    def _():
        for s in (0, 1):
            pl.when(q != s)(lambda: send_bd(0, s).start())
            send_bd(1, s).start()
            send_bd(3, s).start()
        local_b.start()

    @pl.when(jnp.logical_not(own))
    def _():
        send_bp(0).start()
        send_bp(1).start()

    def own_part(p):
        return a_ref.at[:, 0, pl.ds(half * ROWS + p * PROW, PROW), :]

    def part(zz, p):
        return abuf.at[zz, p]

    def turn(j):
        return j + 1 - 2 * (j % 2)

    def a_right(dist, j):
        zz = (z + NZ - dist) % NZ
        return remote(part(zz, j), part(zz, j), s_ar.at[dist, j], r_a.at[zz, j], right)

    def a_left(dist, j):
        zz, p = (z + dist) % NZ, turn(j)
        return remote(part(zz, p), part(zz, p), s_al.at[dist, j], r_a.at[zz, p], left)

    def from_left(dist, j):
        zz = (z + NZ - dist) % NZ
        landed(part(zz, j), r_a.at[zz, j])

    def from_right(dist, j):
        zz, p = (z + dist) % NZ, turn(j)
        landed(part(zz, p), r_a.at[zz, p])

    def local_a(p):
        return pltpu.make_async_copy(own_part(p), part(z, p), s_loc.at[p])

    def start_a(j, carry):
        p = turn(j)
        remote(own_part(j), part(z, j), s_ar.at[0, j], r_a.at[z, j], right).start()
        remote(own_part(p), part(z, p), s_al.at[0, j], r_a.at[z, p], left).start()
        local_a(j).start()
        return carry

    lax.fori_loop(0, PARTS, start_a, 0)

    def send_ia(i):
        return remote(idx_ref, idx_a.at[z], s_ia.at[i], r_ia.at[z], (r, ((z + i) % NZ) * 2 + h, d))

    def send_ib(i):
        yy, core = (y + i // 2) % NY, i % 2
        at = role * NY + y
        return remote(idx_ref, idx_b.at[at], s_ib.at[i], r_ib.at[at], (yy * 2 + core, b_col, b_depth))

    def other_ib(i):
        return jnp.logical_not(own & (i // 2 == 0) & (i % 2 == q))

    send_ic = remote(idx_ref, idx_c, s_ic, r_ic, partner)

    def start_ia(i, carry):
        send_ia(i).start()
        return carry

    def start_ib(i, carry):
        pl.when(other_ib(i))(lambda: send_ib(i).start())
        return carry

    lax.fori_loop(1, NZ, start_ia, 0)
    lax.fori_loop(0, 2 * NY, start_ib, 0)
    send_ic.start()
    idx_a[z] = idx_ref[...]

    @pl.when(own)
    def _():
        idx_b[y] = idx_ref[...]

    acc[...] = jnp.zeros_like(acc)
    for v in range(SPANS):
        for o in (0, 1):
            prods[v, o, ZERO] = jnp.zeros((SROW, BLK), jnp.float32)

    def tables():
        def wait_ia(i, carry):
            zz = (z + i) % NZ
            landed(idx_a.at[zz], r_ia.at[zz])
            return carry

        lax.fori_loop(1, NZ, wait_ia, 0)

        def wait_ib(i, carry):
            yy = (y + i) % NY
            landed(idx_b.at[NY + yy], r_ib.at[NY + yy])
            pl.when(jnp.logical_not(own & (i == 0)))(lambda: landed(idx_b.at[yy], r_ib.at[yy]))
            return carry

        lax.fori_loop(0, NY, wait_ib, 0)
        landed(idx_c, r_ic)

        a_sets = []
        for g in (0, 1):
            rolled = [pltpu.roll(idx_a[g * 4 + i] + 1, i * LANE_A, 1) if i else idx_a[g * 4] + 1 for i in range(4)]
            a_sets.append(rolled[0] + rolled[1] + (rolled[2] + rolled[3]))
        rolled = [pltpu.roll(idx_b[i] + 1, (i // NY) * (BLK // 2) + (i % NY) * BSLOT, 1) if i else idx_b[0] + 1 for i in range(2 * NY)]
        while len(rolled) > 1:
            rolled = [x + w for x, w in zip(rolled[::2], rolled[1::2])]
        b_key, b_to = rolled[0][2:3], rolled[0][3:4]
        a_in = jnp.concatenate([a_sets[0][1:2], a_sets[1][1:2]], axis=1)

        def column(row, count):
            wide = jnp.broadcast_to(row, (count, BLK))
            at = lax.broadcasted_iota(jnp.int32, (count, BLK), 0)
            lane = lax.broadcasted_iota(jnp.int32, (count, BLK), 1)
            return jnp.sum(jnp.where(at == lane, wide, 0), axis=1, keepdims=True)

        key_col = column(b_key, BLK)
        at = lax.broadcasted_iota(jnp.int32, (BLK, 2 * BLK), 0)
        match = (key_col == a_in) & (a_in > 0)
        low_v[...] = jnp.zeros_like(low_v)
        for o in (0, 1):
            mine = match & (at // (BLK // 2) == o)
            first = jnp.min(jnp.where(mine, at % BSLOT, BSLOT), axis=0, keepdims=True)
            last = jnp.max(jnp.where(mine, at % BSLOT, 0), axis=0, keepdims=True)
            low_v[2 * o : 2 * o + 1] = jnp.where(first == BSLOT, 0, first)
            low_v[2 * o + 1 : 2 * o + 2] = last
        at2 = at[:, :BLK]
        lane2 = lax.broadcasted_iota(jnp.int32, (BLK, BLK), 1)
        earlier = (key_col == b_key) & (at2 < lane2) & (at2 // (BLK // 2) == lane2 // (BLK // 2))
        second = jnp.max(jnp.where(earlier, 1, 0), axis=0, keepdims=True)
        row_col = jnp.concatenate([column(a_sets[g][0:1], BLK) for g in (0, 1)], axis=0)
        in_col = jnp.concatenate([column(a_sets[g][1:2], BLK) for g in (0, 1)], axis=0)
        slot = lax.broadcasted_iota(jnp.int32, (2 * BLK, BLK), 0) % LANE_A
        weight = jnp.where((in_col == b_key) & (in_col > 0), slot + 1, 0)
        lane3 = lax.broadcasted_iota(jnp.int32, (CSLOT, BLK), 1)
        mine_c, other_c = idx_ref[...] + 1, idx_c[...] + 1
        for i in (0, 1):
            tab_v[i] = jnp.where(
                lane3 < BLK // 2, column(mine_c[4 + i : 5 + i], CSLOT), column(other_c[4 + i : 5 + i], CSLOT)
            )

        def one_slot(s, carry):
            out_row, out_col = tab_v[0, pl.ds(s, 1)], tab_v[1, pl.ds(s, 1)]
            found = jnp.max(jnp.where(row_col == out_row, weight, 0), axis=0, keepdims=True)
            place = jnp.clip(2 * found - 2 + second, 0, ZERO)
            tab_v[2, pl.ds(s, 1)] = jnp.where((found > 0) & (out_col == b_to), place, ZERO)
            return carry

        lax.fori_loop(0, CSLOT, one_slot, 0)
        for copy in (tab_copy, low_copy):
            copy.start()

    tab_copy = pltpu.make_async_copy(tab_v.at[2], tab_s, s_tab.at[0])
    low_copy = pltpu.make_async_copy(low_v, low_s, s_tab.at[1])

    def spread(o, zz, slot):
        return remote(bbuf.at[o, zz], bbuf.at[o, zz], s_bx.at[slot], r_b.at[o, zz], twin)

    def split_b(o, zz):
        def one(i, carry):
            value = bbuf[o, zz, i]
            high = value.astype(jnp.bfloat16)
            bhi[o, zz, i] = high
            blo[o, zz, i] = (value - high.astype(jnp.float32)).astype(jnp.bfloat16)
            return carry

        lax.fori_loop(0, BSLOT, one, 0)

    def b_slot(i):
        return q * NY + (y + i) % NY

    def b_here(o, i):
        landed(bbuf.at[o, b_slot(i)], r_b.at[o, b_slot(i)])

    def b_next(way):
        zz = b_slot(0)
        return remote(bbuf.at[1, zz], bbuf.at[1, zz], s_bn.at[way], r_b.at[1, zz], (up, down)[way])

    def b_pass(o):
        zz = b_slot(3 if o == 0 else 1)
        return remote(bbuf.at[o, zz], bbuf.at[o, zz], s_bf.at[o], r_b.at[o, zz], (up, down)[o])

    def b_done(o, i):
        spread(o, b_slot(i), i * 2 + o).start()
        split_b(o, b_slot(i))

    def a_step(dist, j):
        from_left(dist, j)
        a_right(dist, j).start()
        from_right(dist, j)
        a_left(dist, j).start()

    a_step(1, 0)
    b_here(0, 0)
    b_done(0, 0)
    a_step(1, 1)
    b_here(1, 0)
    b_next(0).start()
    b_next(1).start()
    b_done(1, 0)
    a_step(1, 2)
    b_here(0, 3)
    b_pass(0).start()
    b_here(0, 1)
    b_done(0, 3)
    b_done(0, 1)
    a_step(1, 3)
    tables()
    b_here(1, 1)
    b_pass(1).start()
    b_here(1, 3)
    b_done(1, 1)
    b_done(1, 3)
    a_step(2, 0)

    def take_b(o, i):
        zz = (1 - q) * NY + (y + i) % NY
        landed(bbuf.at[o, zz], r_b.at[o, zz])
        split_b(o, zz)

    def take_near(k, carry):
        take_b(k // 3, (k % 3 + 3) % NY)
        return carry

    lax.fori_loop(0, 6, take_near, 0)
    a_step(2, 1)
    for p in range(PARTS):
        local_a(p).wait()
    tab_copy.wait()
    low_copy.wait()

    def multiply(zz, first, count, outs):
        rows = count * PROW
        unroll = UNROLL if len(outs) == 2 else UNROLL + UNROLL // 2

        def one(a):
            value = abuf[zz, first : first + count, a].reshape(rows, BLK)
            high = value.astype(jnp.bfloat16)
            low = (value - high.astype(jnp.float32)).astype(jnp.bfloat16)
            twice = [jnp.concatenate([part, part], axis=1) for part in (high, low)]
            both = jnp.concatenate(twice, axis=0)
            for o in outs:
                b0 = low_s[2 * o, zz * LANE_A + a]
                b1 = low_s[2 * o + 1, zz * LANE_A + a]
                wide = jnp.concatenate([bhi[o, zz, b0], bhi[o, zz, b1]], axis=1)
                fine = jnp.concatenate([blo[o, zz, b0], blo[o, zz, b1]], axis=1)
                big = jnp.dot(both, jnp.concatenate([wide, fine], axis=0), preferred_element_type=jnp.float32)
                total = big[:rows] + big[rows:]
                for v in range(rows // SROW):
                    span = first * PROW // SROW + v
                    prods[span, o, 2 * a] = total[v * SROW : (v + 1) * SROW, :BLK]
                    prods[span, o, 2 * a + 1] = total[v * SROW : (v + 1) * SROW, BLK:]

        def some(i, carry):
            for j in range(unroll):
                one(i * unroll + j)
            return carry

        lax.fori_loop(0, ASLOT // unroll, some, 0)

    def gather(zz, o, spans, begin, end):
        base = o * (BLK // 2) + zz * BSLOT

        def some(i, carry):
            for j in range(CSZ):
                s = i * CSZ + j
                at = [tab_s[s, base + b] for b in range(BSLOT)]
                for v in spans:
                    terms = [prods[v, o, p] for p in at]
                    while len(terms) > 1:
                        terms = [x + w for x, w in zip(terms[::2], terms[1::2])]
                    acc[v, o, s] += terms[0]
            return carry

        lax.fori_loop(begin // CSZ, end // CSZ, some, 0)

    offset = (z + NY - y) % NY
    one_first = jnp.where(offset == 2, 1, 0)
    one_second = jnp.where((offset == 1) | (offset == 2), -1, 1)

    def near(k, carry):
        @pl.when(k == 1)
        def _():
            b_here(0, 2)
            b_done(0, 2)
            for j in (2, 3):
                from_left(2, j)
                from_right(2, j)

        @pl.when(k == 2)
        def _():
            b_here(1, 2)
            b_done(1, 2)
            a_step(3, 0)
            for j in (2, 3):
                a_right(2, j).start()
                a_left(2, j).start()
            take_b(0, 2)
            take_b(1, 2)

        third = -one_first - one_second
        by = jnp.where(k == 0, one_first, jnp.where(k == 1, one_second, jnp.where(k == 2, third, 14 - 4 * k)))
        zz = (z + NZ + by) % NZ
        multiply(zz, 0, PARTS, (0, 1))
        for o in (0, 1):
            gather(zz, o, range(SPANS), 0, CSLOT)
        return carry

    lax.fori_loop(0, 5, near, 0)
    from_left(3, 2)
    a_right(3, 2).start()
    from_right(3, 2)
    a_left(3, 2).start()

    def c_piece(v, o, j):
        return acc.at[v, o, pl.ds(j * CSZ, CSZ)]

    def c_landing(v, j):
        return crecv.at[v, pl.ds(j * CSZ, CSZ)]

    def send_c(v, j):
        return remote(c_piece(v, 1, j), c_landing(v, j), s_c.at[v, j], r_c.at[v, j], partner)

    def out_piece(v, j, which):
        return o_ref.at[pl.ds(j * CSZ, CSZ), 0, pl.ds(which * ROWS + v * SROW, SROW), :]

    def send_m(v, j):
        return remote(c_piece(v, 0, j), out_piece(v, j, half), s_m.at[v, j], r_m.at[v, j], mate)

    def store_o(v, j):
        return pltpu.make_async_copy(c_piece(v, 0, j), out_piece(v, j, half), s_o.at[v, j])

    def far(v, o):
        def one(i, carry):
            zz = (z + 3 + 2 * i) % NZ
            multiply(zz, 2 * v, 2, (o,))
            gather(zz, o, (v,), 0, CSLOT)
            return carry

        lax.fori_loop(0, 2, one, 0)

    def finish(v, j):
        landed(c_landing(v, j), r_c.at[v, j])

        def add(s, carry):
            acc[v, 0, s] += crecv[v, s]
            return carry

        lax.fori_loop(j * CSZ, (j + 1) * CSZ, add, 0)
        send_m(v, j).start()
        store_o(v, j).start()

    last = (z + 4) % NZ
    for v in range(SPANS):
        from_left(3, 2 * v + 1)
        from_right(3, 2 * v + 1)
        far(v, 1)
        from_left(4, 2 * v)
        from_right(4, 2 * v)
        multiply(last, 2 * v, 2, (1,))

        def give(j, carry):
            gather(last, 1, (v,), j * CSZ, (j + 1) * CSZ)
            send_c(v, j).start()
            return carry

        lax.fori_loop(0, CCH, give, 0)
        if v:
            finish(0, 2)
            finish(0, 3)
        far(v, 0)
        multiply(last, 2 * v, 2, (0,))
        gather(last, 0, (v,), 0, CSLOT)
        if v == 0:
            finish(0, 0)
            finish(0, 1)
    for j in range(CCH):
        finish(1, j)

    for v in range(SPANS):
        for j in range(CCH):
            landed(out_piece(v, j, 1 - half), r_m.at[v, j])
            store_o(v, j).wait()
            send_m(v, j).wait_send()
            send_c(v, j).wait_send()

    def end_ia(i, carry):
        send_ia(i).wait_send()
        return carry

    def end_ib(i, carry):
        pl.when(other_ib(i))(lambda: send_ib(i).wait_send())
        return carry

    lax.fori_loop(1, NZ, end_ia, 0)
    lax.fori_loop(0, 2 * NY, end_ib, 0)
    send_ic.wait_send()

    @pl.when(own)
    def _():
        for s in (0, 1):
            pl.when(q != s)(lambda: send_bd(0, s).wait_send())
            send_bd(1, s).wait_send()
            send_bd(3, s).wait_send()

    @pl.when(jnp.logical_not(own))
    def _():
        send_bp(0).wait_send()
        send_bp(1).wait_send()

    for o in (0, 1):
        b_next(o).wait_send()
        b_pass(o).wait_send()
        for i in range(NY):
            spread(o, b_slot(i), i * 2 + o).wait_send()

    def end_a(j, carry):
        for dist in range(3):
            a_right(dist, j).wait_send()
            a_left(dist, j).wait_send()

        @pl.when(j % 2 == 0)
        def _():
            a_right(3, j).wait_send()
            a_left(3, j).wait_send()

        return carry

    lax.fori_loop(0, PARTS, end_a, 0)


UNROLL = 8


def index_rows(a_index, b_index, c_index):
    def wide(part):
        return jnp.pad(part, ((0, 0), (0, BLK - part.shape[1])), constant_values=-1)

    b_rows = jnp.pad(b_index[..., 0], ((0, 0), (0, 0), (0, BLK // 4 - BSLOT)), constant_values=-1)
    rows = [a_index[:, :, 0], b_rows.reshape(2, BLK // 2), c_index[:, :, 0], jnp.full((2, BLK), -1, jnp.int32)]
    return jnp.concatenate([wide(part) for part in rows], axis=0)


def local(a_blocks, a_index, b_blocks, b_index, c_index):
    dma = pltpu.SemaphoreType.DMA
    f32, bf16, i32 = jnp.float32, jnp.bfloat16, jnp.int32
    anywhere = pl.BlockSpec(memory_space=pl.ANY)
    return pl.pallas_call(
        kernel,
        out_shape=jax.ShapeDtypeStruct((CSLOT, 1, BLK, BLK), f32),
        in_specs=[pl.BlockSpec(memory_space=pltpu.VMEM), anywhere, anywhere],
        out_specs=anywhere,
        scratch_shapes=[
            pltpu.VMEM((NZ, 8, BLK), i32),
            pltpu.VMEM((2 * NY, 8, BLK), i32),
            pltpu.VMEM((8, BLK), i32),
            pltpu.VMEM((3, CSLOT, BLK), i32),
            pltpu.VMEM((8, 2 * BLK), i32),
            pltpu.SMEM((CSLOT, BLK), i32),
            pltpu.SMEM((8, 2 * BLK), i32),
            pltpu.VMEM((NZ, PARTS, ASLOT, PROW, BLK), f32),
            pltpu.VMEM((2, NZ, BSLOT, BLK, BLK), f32),
            pltpu.VMEM((2, NZ, BSLOT, BLK, BLK), bf16),
            pltpu.VMEM((2, NZ, BSLOT, BLK, BLK), bf16),
            pltpu.VMEM((SPANS, 2, ZERO + 1, SROW, BLK), f32),
            pltpu.VMEM((SPANS, 2, CSLOT, SROW, BLK), f32),
            pltpu.VMEM((SPANS, CSLOT, SROW, BLK), f32),
            dma((NZ,)), dma((NZ,)), dma((2 * NY,)), dma((2 * NY,)), dma, dma, dma((2,)),
            dma((4, PARTS)), dma((4, PARTS)), dma((NZ, PARTS)), dma((PARTS,)),
            dma((NY, 2)), dma((2,)), dma((2,)), dma((2 * NY,)), dma((2, NZ)),
            dma((SPANS, CCH)), dma((SPANS, CCH)), dma((SPANS, CCH)), dma((SPANS, CCH)), dma((SPANS, CCH)),
        ],
        compiler_params=pltpu.CompilerParams(
            collective_id=0, has_side_effects=True, vmem_limit_bytes=56 * 1024 * 1024
        ),
        cost_estimate=pl.CostEstimate(flops=10**10, bytes_accessed=10**7, transcendentals=0),
    )(index_rows(a_index, b_index, c_index), a_blocks, b_blocks)


def solution(mesh):
    in_specs = (
        P("row", "col", None, None),
        P(None, "row", "col"),
        P(None, "row", "col", None, None),
        P(None, None, "row", "col"),
        P(None, "row", "col"),
    )
    out_specs = P("row", "col", None, None)
    return jax.shard_map(local, mesh=mesh, in_specs=in_specs, out_specs=out_specs, check_vma=False)
```

```python
import functools

import jax
import jax.numpy as jnp
from jax import lax
from jax.experimental import pallas as pl
from jax.experimental.pallas import tpu as pltpu
from jax.sharding import PartitionSpec as P

MESH = pl.DeviceIdType.MESH
NZ, NY = 8, 4
ASLOT, BSLOT, CSLOT, BLK = 24, 8, 32, 128
ROWS = BLK // 2
PARTS, PROW = 4, ROWS // 4
SPANS, SROW = 2, ROWS // 2
CCH, CSZ = 4, CSLOT // 4
LANE_A = 32
ZERO = 2 * ASLOT


def kernel(
    idx_ref, a_ref, b_ref, o_ref,
    idx_a, idx_b, idx_c, tab_v, low_v, tab_s, low_s,
    abuf, bbuf, bhi, blo, prods, acc, crecv,
    s_ia, r_ia, s_ib, r_ib, s_ic, r_ic, s_tab,
    s_al, s_ar, r_a, s_loc, s_bd, s_bn, s_bf, s_bx, r_b, s_c, r_c, s_o, s_m, r_m,
):
    r = lax.axis_index("row")
    c = lax.axis_index("col")
    d = lax.axis_index("depth")
    y, q = r // 2, r % 2
    z, h = c // 2, c % 2
    half = (h + d) % 2
    own = q == h
    role = (q + h) % 2
    b_col = z * 2 + q
    b_depth = (d + h + q) % 2
    partner = (r, z * 2 + 1 - h, 1 - d)
    mate = (r, c, 1 - d)
    twin = (y * 2 + 1 - q, c, d)
    up, down = (((y + 1) % NY) * 2 + q, c, d), (((y + 3) % NY) * 2 + q, c, d)
    right, left = (r, ((z + 1) % NZ) * 2 + h, d), (r, ((z + 7) % NZ) * 2 + h, d)

    def remote(src, dst, send, recv, device):
        return pltpu.make_async_remote_copy(
            src_ref=src, dst_ref=dst, send_sem=send, recv_sem=recv, device_id=device, device_id_type=MESH
        )

    def landed(ref, sem):
        pltpu.make_async_copy(ref, ref, sem).wait()

    barrier = pltpu.get_barrier_semaphore()

    def greet(device):
        pl.semaphore_signal(barrier, inc=1, device_id=device, device_id_type=MESH)

    def greet_z(i, carry):
        greet((r, ((z + i) % NZ) * 2 + h, d))
        return carry

    lax.fori_loop(1, NZ, greet_z, 0)

    def greet_b(i, carry):
        yy = (y + i) % NY
        greet((yy * 2 + h, z * 2 + 1 - h, 1 - d))

        @pl.when(jnp.logical_not(own & (i == 0)))
        def _():
            greet((yy * 2 + h, c, d))

        return carry

    lax.fori_loop(0, NY, greet_b, 0)
    for device in (partner, mate, twin, up, down):
        greet(device)
    pl.semaphore_wait(barrier, NZ - 1 + 2 * NY + 5 - own.astype(jnp.int32))

    def send_bd(i, s):
        yy = (y + i) % NY
        return remote(b_ref.at[s, :, 0], bbuf.at[0, s * NY + y], s_bd.at[i, s], r_b.at[0, s * NY + y], (yy * 2 + s, c, d))

    def send_bp(s):
        return remote(
            b_ref.at[s, :, 0], bbuf.at[1, s * NY + y], s_bd.at[0, s], r_b.at[1, s * NY + y],
            (y * 2 + s, z * 2 + 1 - h, 1 - d),
        )

    local_b = pltpu.make_async_copy(b_ref.at[q, :, 0], bbuf.at[0, q * NY + y], r_b.at[0, q * NY + y])

    @pl.when(own)
    def _():
        for s in (0, 1):
            pl.when(q != s)(lambda: send_bd(0, s).start())
            send_bd(1, s).start()
            send_bd(3, s).start()
        local_b.start()

    @pl.when(jnp.logical_not(own))
    def _():
        send_bp(0).start()
        send_bp(1).start()

    def own_part(p):
        return a_ref.at[:, 0, pl.ds(half * ROWS + p * PROW, PROW), :]

    def part(zz, p):
        return abuf.at[zz, p]

    def turn(j):
        return j + 1 - 2 * (j % 2)

    def a_right(dist, j):
        zz = (z + NZ - dist) % NZ
        return remote(part(zz, j), part(zz, j), s_ar.at[dist, j], r_a.at[zz, j], right)

    def a_left(dist, j):
        zz, p = (z + dist) % NZ, turn(j)
        return remote(part(zz, p), part(zz, p), s_al.at[dist, j], r_a.at[zz, p], left)

    def from_left(dist, j):
        zz = (z + NZ - dist) % NZ
        landed(part(zz, j), r_a.at[zz, j])

    def from_right(dist, j):
        zz, p = (z + dist) % NZ, turn(j)
        landed(part(zz, p), r_a.at[zz, p])

    def local_a(p):
        return pltpu.make_async_copy(own_part(p), part(z, p), s_loc.at[p])

    def start_a(j, carry):
        p = turn(j)
        remote(own_part(j), part(z, j), s_ar.at[0, j], r_a.at[z, j], right).start()
        remote(own_part(p), part(z, p), s_al.at[0, j], r_a.at[z, p], left).start()
        local_a(j).start()
        return carry

    lax.fori_loop(0, PARTS, start_a, 0)

    def send_ia(i):
        return remote(idx_ref, idx_a.at[z], s_ia.at[i], r_ia.at[z], (r, ((z + i) % NZ) * 2 + h, d))

    def send_ib(i):
        yy, core = (y + i // 2) % NY, i % 2
        at = role * NY + y
        return remote(idx_ref, idx_b.at[at], s_ib.at[i], r_ib.at[at], (yy * 2 + core, b_col, b_depth))

    def other_ib(i):
        return jnp.logical_not(own & (i // 2 == 0) & (i % 2 == q))

    send_ic = remote(idx_ref, idx_c, s_ic, r_ic, partner)

    def start_ia(i, carry):
        send_ia(i).start()
        return carry

    def start_ib(i, carry):
        pl.when(other_ib(i))(lambda: send_ib(i).start())
        return carry

    lax.fori_loop(1, NZ, start_ia, 0)
    lax.fori_loop(0, 2 * NY, start_ib, 0)
    send_ic.start()
    idx_a[z] = idx_ref[...]

    @pl.when(own)
    def _():
        idx_b[y] = idx_ref[...]

    acc[...] = jnp.zeros_like(acc)
    for v in range(SPANS):
        for o in (0, 1):
            prods[v, o, ZERO] = jnp.zeros((SROW, BLK), jnp.float32)

    def tables():
        def wait_ia(i, carry):
            zz = (z + i) % NZ
            landed(idx_a.at[zz], r_ia.at[zz])
            return carry

        lax.fori_loop(1, NZ, wait_ia, 0)

        def wait_ib(i, carry):
            yy = (y + i) % NY
            landed(idx_b.at[NY + yy], r_ib.at[NY + yy])
            pl.when(jnp.logical_not(own & (i == 0)))(lambda: landed(idx_b.at[yy], r_ib.at[yy]))
            return carry

        lax.fori_loop(0, NY, wait_ib, 0)
        landed(idx_c, r_ic)

        a_sets = []
        for g in (0, 1):
            rolled = [pltpu.roll(idx_a[g * 4 + i] + 1, i * LANE_A, 1) if i else idx_a[g * 4] + 1 for i in range(4)]
            a_sets.append(rolled[0] + rolled[1] + (rolled[2] + rolled[3]))
        rolled = [pltpu.roll(idx_b[i] + 1, (i // NY) * (BLK // 2) + (i % NY) * BSLOT, 1) if i else idx_b[0] + 1 for i in range(2 * NY)]
        while len(rolled) > 1:
            rolled = [x + w for x, w in zip(rolled[::2], rolled[1::2])]
        b_key, b_to = rolled[0][2:3], rolled[0][3:4]
        a_in = jnp.concatenate([a_sets[0][1:2], a_sets[1][1:2]], axis=1)

        def column(row, count):
            wide = jnp.broadcast_to(row, (count, BLK))
            at = lax.broadcasted_iota(jnp.int32, (count, BLK), 0)
            lane = lax.broadcasted_iota(jnp.int32, (count, BLK), 1)
            return jnp.sum(jnp.where(at == lane, wide, 0), axis=1, keepdims=True)

        key_col = column(b_key, BLK)
        at = lax.broadcasted_iota(jnp.int32, (BLK, 2 * BLK), 0)
        match = (key_col == a_in) & (a_in > 0)
        low_v[...] = jnp.zeros_like(low_v)
        for o in (0, 1):
            mine = match & (at // (BLK // 2) == o)
            first = jnp.min(jnp.where(mine, at % BSLOT, BSLOT), axis=0, keepdims=True)
            last = jnp.max(jnp.where(mine, at % BSLOT, 0), axis=0, keepdims=True)
            low_v[2 * o : 2 * o + 1] = jnp.where(first == BSLOT, 0, first)
            low_v[2 * o + 1 : 2 * o + 2] = last
        at2 = at[:, :BLK]
        lane2 = lax.broadcasted_iota(jnp.int32, (BLK, BLK), 1)
        earlier = (key_col == b_key) & (at2 < lane2) & (at2 // (BLK // 2) == lane2 // (BLK // 2))
        second = jnp.max(jnp.where(earlier, 1, 0), axis=0, keepdims=True)
        row_col = jnp.concatenate([column(a_sets[g][0:1], BLK) for g in (0, 1)], axis=0)
        in_col = jnp.concatenate([column(a_sets[g][1:2], BLK) for g in (0, 1)], axis=0)
        slot = lax.broadcasted_iota(jnp.int32, (2 * BLK, BLK), 0) % LANE_A
        weight = jnp.where((in_col == b_key) & (in_col > 0), slot + 1, 0)
        lane3 = lax.broadcasted_iota(jnp.int32, (CSLOT, BLK), 1)
        mine_c, other_c = idx_ref[...] + 1, idx_c[...] + 1
        for i in (0, 1):
            tab_v[i] = jnp.where(
                lane3 < BLK // 2, column(mine_c[4 + i : 5 + i], CSLOT), column(other_c[4 + i : 5 + i], CSLOT)
            )

        def one_slot(s, carry):
            out_row, out_col = tab_v[0, pl.ds(s, 1)], tab_v[1, pl.ds(s, 1)]
            found = jnp.max(jnp.where(row_col == out_row, weight, 0), axis=0, keepdims=True)
            place = jnp.clip(2 * found - 2 + second, 0, ZERO)
            tab_v[2, pl.ds(s, 1)] = jnp.where((found > 0) & (out_col == b_to), place, ZERO)
            return carry

        lax.fori_loop(0, CSLOT, one_slot, 0)
        for copy in (tab_copy, low_copy):
            copy.start()

    tab_copy = pltpu.make_async_copy(tab_v.at[2], tab_s, s_tab.at[0])
    low_copy = pltpu.make_async_copy(low_v, low_s, s_tab.at[1])

    def spread(o, zz, slot):
        return remote(bbuf.at[o, zz], bbuf.at[o, zz], s_bx.at[slot], r_b.at[o, zz], twin)

    def split_b(o, zz):
        def one(i, carry):
            value = bbuf[o, zz, i]
            high = value.astype(jnp.bfloat16)
            bhi[o, zz, i] = high
            blo[o, zz, i] = (value - high.astype(jnp.float32)).astype(jnp.bfloat16)
            return carry

        lax.fori_loop(0, BSLOT, one, 0)

    def b_slot(i):
        return q * NY + (y + i) % NY

    def b_here(o, i):
        landed(bbuf.at[o, b_slot(i)], r_b.at[o, b_slot(i)])

    def b_next(way):
        zz = b_slot(0)
        return remote(bbuf.at[1, zz], bbuf.at[1, zz], s_bn.at[way], r_b.at[1, zz], (up, down)[way])

    def b_pass(o):
        zz = b_slot(3 if o == 0 else 1)
        return remote(bbuf.at[o, zz], bbuf.at[o, zz], s_bf.at[o], r_b.at[o, zz], (up, down)[o])

    def b_done(o, i):
        spread(o, b_slot(i), i * 2 + o).start()
        split_b(o, b_slot(i))

    def a_step(dist, j):
        from_left(dist, j)
        a_right(dist, j).start()
        from_right(dist, j)
        a_left(dist, j).start()

    a_step(1, 0)
    b_here(0, 0)
    b_done(0, 0)
    a_step(1, 1)
    b_here(1, 0)
    b_next(0).start()
    b_next(1).start()
    b_done(1, 0)
    a_step(1, 2)
    b_here(0, 3)
    b_pass(0).start()
    b_here(0, 1)
    b_done(0, 3)
    b_done(0, 1)
    a_step(1, 3)
    tables()
    b_here(1, 1)
    b_pass(1).start()
    b_here(1, 3)
    b_done(1, 1)
    b_done(1, 3)
    a_step(2, 0)

    def take_b(o, i):
        zz = (1 - q) * NY + (y + i) % NY
        landed(bbuf.at[o, zz], r_b.at[o, zz])
        split_b(o, zz)

    def take_near(k, carry):
        take_b(k // 3, (k % 3 + 3) % NY)
        return carry

    lax.fori_loop(0, 6, take_near, 0)
    a_step(2, 1)
    for p in range(PARTS):
        local_a(p).wait()
    tab_copy.wait()
    low_copy.wait()

    def multiply(zz, first, count, outs):
        rows = count * PROW
        unroll = UNROLL if len(outs) == 2 else UNROLL + UNROLL // 2

        def one(a):
            value = abuf[zz, first : first + count, a].reshape(rows, BLK)
            high = value.astype(jnp.bfloat16)
            low = (value - high.astype(jnp.float32)).astype(jnp.bfloat16)
            twice = [jnp.concatenate([part, part], axis=1) for part in (high, low)]
            both = jnp.concatenate(twice, axis=0)
            for o in outs:
                b0 = low_s[2 * o, zz * LANE_A + a]
                b1 = low_s[2 * o + 1, zz * LANE_A + a]
                wide = jnp.concatenate([bhi[o, zz, b0], bhi[o, zz, b1]], axis=1)
                fine = jnp.concatenate([blo[o, zz, b0], blo[o, zz, b1]], axis=1)
                big = jnp.dot(both, jnp.concatenate([wide, fine], axis=0), preferred_element_type=jnp.float32)
                total = big[:rows] + big[rows:]
                for v in range(rows // SROW):
                    span = first * PROW // SROW + v
                    prods[span, o, 2 * a] = total[v * SROW : (v + 1) * SROW, :BLK]
                    prods[span, o, 2 * a + 1] = total[v * SROW : (v + 1) * SROW, BLK:]

        def some(i, carry):
            for j in range(unroll):
                one(i * unroll + j)
            return carry

        lax.fori_loop(0, ASLOT // unroll, some, 0)

    def gather(zz, o, spans, begin, end):
        base = o * (BLK // 2) + zz * BSLOT

        def some(i, carry):
            for j in range(CSZ):
                s = i * CSZ + j
                at = [tab_s[s, base + b] for b in range(BSLOT)]
                for v in spans:
                    terms = [prods[v, o, p] for p in at]
                    while len(terms) > 1:
                        terms = [x + w for x, w in zip(terms[::2], terms[1::2])]
                    acc[v, o, s] += terms[0]
            return carry

        lax.fori_loop(begin // CSZ, end // CSZ, some, 0)

    offset = (z + NY - y) % NY
    one_first = jnp.where(offset == 2, 1, 0)
    one_second = jnp.where((offset == 1) | (offset == 2), -1, 1)

    def near(k, carry):
        @pl.when(k == 1)
        def _():
            b_here(0, 2)
            b_done(0, 2)
            for j in (2, 3):
                from_left(2, j)
                from_right(2, j)

        @pl.when(k == 2)
        def _():
            b_here(1, 2)
            b_done(1, 2)
            a_step(3, 0)
            for j in (2, 3):
                a_right(2, j).start()
                a_left(2, j).start()
            take_b(0, 2)
            take_b(1, 2)

        third = -one_first - one_second
        by = jnp.where(k == 0, one_first, jnp.where(k == 1, one_second, jnp.where(k == 2, third, 14 - 4 * k)))
        zz = (z + NZ + by) % NZ
        multiply(zz, 0, PARTS, (0, 1))
        for o in (0, 1):
            gather(zz, o, range(SPANS), 0, CSLOT)
        return carry

    lax.fori_loop(0, 5, near, 0)
    from_left(3, 2)
    a_right(3, 2).start()
    from_right(3, 2)
    a_left(3, 2).start()

    def c_piece(v, o, j):
        return acc.at[v, o, pl.ds(j * CSZ, CSZ)]

    def c_landing(v, j):
        return crecv.at[v, pl.ds(j * CSZ, CSZ)]

    def send_c(v, j):
        return remote(c_piece(v, 1, j), c_landing(v, j), s_c.at[v, j], r_c.at[v, j], partner)

    def out_piece(v, j, which):
        return o_ref.at[pl.ds(j * CSZ, CSZ), 0, pl.ds(which * ROWS + v * SROW, SROW), :]

    def send_m(v, j):
        return remote(c_piece(v, 0, j), out_piece(v, j, half), s_m.at[v, j], r_m.at[v, j], mate)

    def store_o(v, j):
        return pltpu.make_async_copy(c_piece(v, 0, j), out_piece(v, j, half), s_o.at[v, j])

    def far(v, o):
        def one(i, carry):
            zz = (z + 3 + 2 * i) % NZ
            multiply(zz, 2 * v, 2, (o,))
            gather(zz, o, (v,), 0, CSLOT)
            return carry

        lax.fori_loop(0, 2, one, 0)

    def finish(v, j):
        landed(c_landing(v, j), r_c.at[v, j])

        def add(s, carry):
            acc[v, 0, s] += crecv[v, s]
            return carry

        lax.fori_loop(j * CSZ, (j + 1) * CSZ, add, 0)
        send_m(v, j).start()
        store_o(v, j).start()

    last = (z + 4) % NZ

    def give(v):
        from_left(4, 2 * v)
        from_right(4, 2 * v)
        multiply(last, 2 * v, 2, (1,))

        def one(j, carry):
            gather(last, 1, (v,), j * CSZ, (j + 1) * CSZ)
            send_c(v, j).start()
            return carry

        lax.fori_loop(0, CCH, one, 0)

    def keep(v):
        multiply(last, 2 * v, 2, (0,))
        gather(last, 0, (v,), 0, CSLOT)

    from_left(3, 1)
    from_right(3, 1)
    far(0, 1)
    give(0)
    far(0, 0)
    keep(0)
    finish(0, 0)
    from_left(3, 3)
    from_right(3, 3)
    far(1, 1)
    finish(0, 1)
    give(1)
    finish(0, 2)
    far(1, 0)
    finish(0, 3)
    keep(1)
    for j in range(CCH):
        finish(1, j)

    for v in range(SPANS):
        for j in range(CCH):
            landed(out_piece(v, j, 1 - half), r_m.at[v, j])
            store_o(v, j).wait()
            send_m(v, j).wait_send()
            send_c(v, j).wait_send()

    def end_ia(i, carry):
        send_ia(i).wait_send()
        return carry

    def end_ib(i, carry):
        pl.when(other_ib(i))(lambda: send_ib(i).wait_send())
        return carry

    lax.fori_loop(1, NZ, end_ia, 0)
    lax.fori_loop(0, 2 * NY, end_ib, 0)
    send_ic.wait_send()

    @pl.when(own)
    def _():
        for s in (0, 1):
            pl.when(q != s)(lambda: send_bd(0, s).wait_send())
            send_bd(1, s).wait_send()
            send_bd(3, s).wait_send()

    @pl.when(jnp.logical_not(own))
    def _():
        send_bp(0).wait_send()
        send_bp(1).wait_send()

    for o in (0, 1):
        b_next(o).wait_send()
        b_pass(o).wait_send()
        for i in range(NY):
            spread(o, b_slot(i), i * 2 + o).wait_send()

    def end_a(j, carry):
        for dist in range(3):
            a_right(dist, j).wait_send()
            a_left(dist, j).wait_send()

        @pl.when(j % 2 == 0)
        def _():
            a_right(3, j).wait_send()
            a_left(3, j).wait_send()

        return carry

    lax.fori_loop(0, PARTS, end_a, 0)


UNROLL = 8


def index_rows(a_index, b_index, c_index):
    def place(part, row, lane):
        rows, lanes = part.shape
        return lax.pad(part, jnp.int32(-1), ((row, 8 - row - rows, 0), (lane, BLK - lane - lanes, 0)))

    ours = jnp.maximum(place(a_index[:, :, 0], 0, 0), place(b_index[:, 0, :, 0], 2, 0))
    ours = jnp.maximum(ours, place(b_index[:, 1, :, 0], 2, BLK // 4))
    return jnp.maximum(ours, place(c_index[:, :, 0], 4, 0))


def local(a_blocks, a_index, b_blocks, b_index, c_index):
    dma = pltpu.SemaphoreType.DMA
    f32, bf16, i32 = jnp.float32, jnp.bfloat16, jnp.int32
    anywhere, outside = pl.BlockSpec(memory_space=pl.ANY), pl.BlockSpec(memory_space=pltpu.HBM)
    return pl.pallas_call(
        kernel,
        out_shape=jax.ShapeDtypeStruct((CSLOT, 1, BLK, BLK), f32),
        in_specs=[pl.BlockSpec(memory_space=pltpu.VMEM), outside, outside],
        out_specs=anywhere,
        scratch_shapes=[
            pltpu.VMEM((NZ, 8, BLK), i32),
            pltpu.VMEM((2 * NY, 8, BLK), i32),
            pltpu.VMEM((8, BLK), i32),
            pltpu.VMEM((3, CSLOT, BLK), i32),
            pltpu.VMEM((8, 2 * BLK), i32),
            pltpu.SMEM((CSLOT, BLK), i32),
            pltpu.SMEM((8, 2 * BLK), i32),
            pltpu.VMEM((NZ, PARTS, ASLOT, PROW, BLK), f32),
            pltpu.VMEM((2, NZ, BSLOT, BLK, BLK), f32),
            pltpu.VMEM((2, NZ, BSLOT, BLK, BLK), bf16),
            pltpu.VMEM((2, NZ, BSLOT, BLK, BLK), bf16),
            pltpu.VMEM((SPANS, 2, ZERO + 1, SROW, BLK), f32),
            pltpu.VMEM((SPANS, 2, CSLOT, SROW, BLK), f32),
            pltpu.VMEM((SPANS, CSLOT, SROW, BLK), f32),
            dma((NZ,)), dma((NZ,)), dma((2 * NY,)), dma((2 * NY,)), dma, dma, dma((2,)),
            dma((4, PARTS)), dma((4, PARTS)), dma((NZ, PARTS)), dma((PARTS,)),
            dma((NY, 2)), dma((2,)), dma((2,)), dma((2 * NY,)), dma((2, NZ)),
            dma((SPANS, CCH)), dma((SPANS, CCH)), dma((SPANS, CCH)), dma((SPANS, CCH)), dma((SPANS, CCH)),
        ],
        compiler_params=pltpu.CompilerParams(
            collective_id=0, has_side_effects=True, vmem_limit_bytes=36 * 1024 * 1024
        ),
        cost_estimate=pl.CostEstimate(flops=10**10, bytes_accessed=10**7, transcendentals=0),
    )(index_rows(a_index, b_index, c_index), a_blocks, b_blocks)


def solution(mesh):
    in_specs = (
        P("row", "col", None, None),
        P(None, "row", "col"),
        P(None, "row", "col", None, None),
        P(None, None, "row", "col"),
        P(None, "row", "col"),
    )
    out_specs = P("row", "col", None, None)
    return jax.shard_map(local, mesh=mesh, in_specs=in_specs, out_specs=out_specs, check_vma=False)
```

```python
import functools

import jax
import jax.numpy as jnp
from jax import lax
from jax.experimental import pallas as pl
from jax.experimental.pallas import tpu as pltpu
from jax.sharding import PartitionSpec as P

MESH = pl.DeviceIdType.MESH
NZ, NY = 8, 4
ASLOT, BSLOT, CSLOT, BLK = 24, 8, 32, 128
ROWS = BLK // 2
PARTS, PROW = 4, ROWS // 4
SPANS, SROW = 2, ROWS // 2
CCH, CSZ = 4, CSLOT // 4
LANE_A = 32
ZERO = 2 * ASLOT


def kernel(
    idx_ref, a_ref, b_ref, o_ref,
    idx_a, idx_b, idx_c, tab_v, low_v, tab_s, low_s,
    abuf, bbuf, bhi, blo, prods, acc, crecv,
    s_ia, r_ia, s_ib, r_ib, s_ic, r_ic, s_tab,
    s_al, s_ar, r_a, s_loc, s_bd, s_bn, s_bf, s_bx, r_b, s_c, r_c, s_o, s_m, r_m, hello,
):
    r = lax.axis_index("row")
    c = lax.axis_index("col")
    d = lax.axis_index("depth")
    y, q = r // 2, r % 2
    z, h = c // 2, c % 2
    half = (h + d) % 2
    own = q == h
    role = (q + h) % 2
    b_col = z * 2 + q
    b_depth = (d + h + q) % 2
    partner = (r, z * 2 + 1 - h, 1 - d)
    mate = (r, c, 1 - d)
    twin = (y * 2 + 1 - q, c, d)
    up, down = (((y + 1) % NY) * 2 + q, c, d), (((y + 3) % NY) * 2 + q, c, d)
    right, left = (r, ((z + 1) % NZ) * 2 + h, d), (r, ((z + 7) % NZ) * 2 + h, d)

    def remote(src, dst, send, recv, device):
        return pltpu.make_async_remote_copy(
            src_ref=src, dst_ref=dst, send_sem=send, recv_sem=recv, device_id=device, device_id_type=MESH
        )

    def landed(ref, sem):
        pltpu.make_async_copy(ref, ref, sem).wait()

    barrier = pltpu.get_barrier_semaphore()
    near_by = [right, left, up, down, twin, partner, mate]
    near_by += [(((y + i) % NY) * 2 + 1 - q, c, d) for i in (1, 3)]
    near_by += [(y * 2 + 1 - q, z * 2 + 1 - h, 1 - d)]
    for device in near_by:
        pl.semaphore_signal(barrier, inc=1, device_id=device, device_id_type=MESH)
    pl.semaphore_wait(barrier, len(near_by))

    def send_bd(i, s):
        yy = (y + i) % NY
        return remote(b_ref.at[s, :, 0], bbuf.at[0, s * NY + y], s_bd.at[i, s], r_b.at[0, s * NY + y], (yy * 2 + s, c, d))

    def send_bp(s):
        return remote(
            b_ref.at[s, :, 0], bbuf.at[1, s * NY + y], s_bd.at[0, s], r_b.at[1, s * NY + y],
            (y * 2 + s, z * 2 + 1 - h, 1 - d),
        )

    local_b = pltpu.make_async_copy(b_ref.at[q, :, 0], bbuf.at[0, q * NY + y], r_b.at[0, q * NY + y])

    @pl.when(own)
    def _():
        for s in (0, 1):
            pl.when(q != s)(lambda: send_bd(0, s).start())
            send_bd(1, s).start()
            send_bd(3, s).start()
        local_b.start()

    @pl.when(jnp.logical_not(own))
    def _():
        send_bp(0).start()
        send_bp(1).start()

    def own_part(p):
        return a_ref.at[:, 0, pl.ds(half * ROWS + p * PROW, PROW), :]

    def part(zz, p):
        return abuf.at[zz, p]

    def turn(j):
        return j + 1 - 2 * (j % 2)

    def a_right(dist, j):
        zz = (z + NZ - dist) % NZ
        return remote(part(zz, j), part(zz, j), s_ar.at[dist, j], r_a.at[zz, j], right)

    def a_left(dist, j):
        zz, p = (z + dist) % NZ, turn(j)
        return remote(part(zz, p), part(zz, p), s_al.at[dist, j], r_a.at[zz, p], left)

    def from_left(dist, j):
        zz = (z + NZ - dist) % NZ
        landed(part(zz, j), r_a.at[zz, j])

    def from_right(dist, j):
        zz, p = (z + dist) % NZ, turn(j)
        landed(part(zz, p), r_a.at[zz, p])

    def local_a(p):
        return pltpu.make_async_copy(own_part(p), part(z, p), s_loc.at[p])

    def start_a(j, carry):
        p = turn(j)
        remote(own_part(j), part(z, j), s_ar.at[0, j], r_a.at[z, j], right).start()
        remote(own_part(p), part(z, p), s_al.at[0, j], r_a.at[z, p], left).start()
        local_a(j).start()
        return carry

    lax.fori_loop(0, PARTS, start_a, 0)

    for n in range(ROUNDS):
        for device in near_by:
            pl.semaphore_signal(hello.at[n], inc=1, device_id=device, device_id_type=MESH)
        pl.semaphore_wait(hello.at[n], len(near_by))

    def send_ia(i):
        return remote(idx_ref, idx_a.at[z], s_ia.at[i], r_ia.at[z], (r, ((z + i) % NZ) * 2 + h, d))

    def send_ib(i):
        yy, core = (y + i // 2) % NY, i % 2
        at = role * NY + y
        return remote(idx_ref, idx_b.at[at], s_ib.at[i], r_ib.at[at], (yy * 2 + core, b_col, b_depth))

    def other_ib(i):
        return jnp.logical_not(own & (i // 2 == 0) & (i % 2 == q))

    send_ic = remote(idx_ref, idx_c, s_ic, r_ic, partner)

    def start_ia(i, carry):
        send_ia(i).start()
        return carry

    def start_ib(i, carry):
        pl.when(other_ib(i))(lambda: send_ib(i).start())
        return carry

    lax.fori_loop(1, NZ, start_ia, 0)
    lax.fori_loop(0, 2 * NY, start_ib, 0)
    send_ic.start()
    idx_a[z] = idx_ref[...]

    @pl.when(own)
    def _():
        idx_b[y] = idx_ref[...]

    acc[...] = jnp.zeros_like(acc)
    for v in range(SPANS):
        for o in (0, 1):
            prods[v, o, ZERO] = jnp.zeros((SROW, BLK), jnp.float32)

    def tables():
        def wait_ia(i, carry):
            zz = (z + i) % NZ
            landed(idx_a.at[zz], r_ia.at[zz])
            return carry

        lax.fori_loop(1, NZ, wait_ia, 0)

        def wait_ib(i, carry):
            yy = (y + i) % NY
            landed(idx_b.at[NY + yy], r_ib.at[NY + yy])
            pl.when(jnp.logical_not(own & (i == 0)))(lambda: landed(idx_b.at[yy], r_ib.at[yy]))
            return carry

        lax.fori_loop(0, NY, wait_ib, 0)
        landed(idx_c, r_ic)

        a_sets = []
        for g in (0, 1):
            rolled = [pltpu.roll(idx_a[g * 4 + i] + 1, i * LANE_A, 1) if i else idx_a[g * 4] + 1 for i in range(4)]
            a_sets.append(rolled[0] + rolled[1] + (rolled[2] + rolled[3]))
        rolled = [pltpu.roll(idx_b[i] + 1, (i // NY) * (BLK // 2) + (i % NY) * BSLOT, 1) if i else idx_b[0] + 1 for i in range(2 * NY)]
        while len(rolled) > 1:
            rolled = [x + w for x, w in zip(rolled[::2], rolled[1::2])]
        b_key, b_to = rolled[0][2:3], rolled[0][3:4]
        a_in = jnp.concatenate([a_sets[0][1:2], a_sets[1][1:2]], axis=1)

        def column(row, count):
            wide = jnp.broadcast_to(row, (count, BLK))
            at = lax.broadcasted_iota(jnp.int32, (count, BLK), 0)
            lane = lax.broadcasted_iota(jnp.int32, (count, BLK), 1)
            return jnp.sum(jnp.where(at == lane, wide, 0), axis=1, keepdims=True)

        key_col = column(b_key, BLK)
        at = lax.broadcasted_iota(jnp.int32, (BLK, 2 * BLK), 0)
        match = (key_col == a_in) & (a_in > 0)
        low_v[...] = jnp.zeros_like(low_v)
        for o in (0, 1):
            mine = match & (at // (BLK // 2) == o)
            first = jnp.min(jnp.where(mine, at % BSLOT, BSLOT), axis=0, keepdims=True)
            last = jnp.max(jnp.where(mine, at % BSLOT, 0), axis=0, keepdims=True)
            low_v[2 * o : 2 * o + 1] = jnp.where(first == BSLOT, 0, first)
            low_v[2 * o + 1 : 2 * o + 2] = last
        at2 = at[:, :BLK]
        lane2 = lax.broadcasted_iota(jnp.int32, (BLK, BLK), 1)
        earlier = (key_col == b_key) & (at2 < lane2) & (at2 // (BLK // 2) == lane2 // (BLK // 2))
        second = jnp.max(jnp.where(earlier, 1, 0), axis=0, keepdims=True)
        row_col = jnp.concatenate([column(a_sets[g][0:1], BLK) for g in (0, 1)], axis=0)
        in_col = jnp.concatenate([column(a_sets[g][1:2], BLK) for g in (0, 1)], axis=0)
        slot = lax.broadcasted_iota(jnp.int32, (2 * BLK, BLK), 0) % LANE_A
        weight = jnp.where((in_col == b_key) & (in_col > 0), slot + 1, 0)
        lane3 = lax.broadcasted_iota(jnp.int32, (CSLOT, BLK), 1)
        mine_c, other_c = idx_ref[...] + 1, idx_c[...] + 1
        for i in (0, 1):
            tab_v[i] = jnp.where(
                lane3 < BLK // 2, column(mine_c[4 + i : 5 + i], CSLOT), column(other_c[4 + i : 5 + i], CSLOT)
            )

        def one_slot(s, carry):
            out_row, out_col = tab_v[0, pl.ds(s, 1)], tab_v[1, pl.ds(s, 1)]
            found = jnp.max(jnp.where(row_col == out_row, weight, 0), axis=0, keepdims=True)
            place = jnp.clip(2 * found - 2 + second, 0, ZERO)
            tab_v[2, pl.ds(s, 1)] = jnp.where((found > 0) & (out_col == b_to), place, ZERO)
            return carry

        lax.fori_loop(0, CSLOT, one_slot, 0)
        for copy in (tab_copy, low_copy):
            copy.start()

    tab_copy = pltpu.make_async_copy(tab_v.at[2], tab_s, s_tab.at[0])
    low_copy = pltpu.make_async_copy(low_v, low_s, s_tab.at[1])

    def spread(o, zz, slot):
        return remote(bbuf.at[o, zz], bbuf.at[o, zz], s_bx.at[slot], r_b.at[o, zz], twin)

    def split_b(o, zz):
        def one(i, carry):
            value = bbuf[o, zz, i]
            high = value.astype(jnp.bfloat16)
            bhi[o, zz, i] = high
            blo[o, zz, i] = (value - high.astype(jnp.float32)).astype(jnp.bfloat16)
            return carry

        lax.fori_loop(0, BSLOT, one, 0)

    def b_slot(i):
        return q * NY + (y + i) % NY

    def b_here(o, i):
        landed(bbuf.at[o, b_slot(i)], r_b.at[o, b_slot(i)])

    def b_next(way):
        zz = b_slot(0)
        return remote(bbuf.at[1, zz], bbuf.at[1, zz], s_bn.at[way], r_b.at[1, zz], (up, down)[way])

    def b_pass(o):
        zz = b_slot(3 if o == 0 else 1)
        return remote(bbuf.at[o, zz], bbuf.at[o, zz], s_bf.at[o], r_b.at[o, zz], (up, down)[o])

    def b_done(o, i):
        spread(o, b_slot(i), i * 2 + o).start()
        split_b(o, b_slot(i))

    def a_step(dist, j):
        from_left(dist, j)
        a_right(dist, j).start()
        from_right(dist, j)
        a_left(dist, j).start()

    a_step(1, 0)
    b_here(0, 0)
    b_done(0, 0)
    a_step(1, 1)
    b_here(1, 0)
    b_next(0).start()
    b_next(1).start()
    b_done(1, 0)
    a_step(1, 2)
    b_here(0, 3)
    b_pass(0).start()
    b_here(0, 1)
    b_done(0, 3)
    b_done(0, 1)
    a_step(1, 3)
    tables()
    b_here(1, 1)
    b_pass(1).start()
    b_here(1, 3)
    b_done(1, 1)
    b_done(1, 3)
    a_step(2, 0)

    def take_b(o, i):
        zz = (1 - q) * NY + (y + i) % NY
        landed(bbuf.at[o, zz], r_b.at[o, zz])
        split_b(o, zz)

    def take_near(k, carry):
        take_b(k // 3, (k % 3 + 3) % NY)
        return carry

    lax.fori_loop(0, 6, take_near, 0)
    a_step(2, 1)
    for p in range(PARTS):
        local_a(p).wait()
    tab_copy.wait()
    low_copy.wait()

    def multiply(zz, first, count, outs):
        rows = count * PROW
        unroll = UNROLL if len(outs) == 2 else UNROLL + UNROLL // 2

        def one(a):
            value = abuf[zz, first : first + count, a].reshape(rows, BLK)
            high = value.astype(jnp.bfloat16)
            low = (value - high.astype(jnp.float32)).astype(jnp.bfloat16)
            twice = [jnp.concatenate([part, part], axis=1) for part in (high, low)]
            both = jnp.concatenate(twice, axis=0)
            for o in outs:
                b0 = low_s[2 * o, zz * LANE_A + a]
                b1 = low_s[2 * o + 1, zz * LANE_A + a]
                wide = jnp.concatenate([bhi[o, zz, b0], bhi[o, zz, b1]], axis=1)
                fine = jnp.concatenate([blo[o, zz, b0], blo[o, zz, b1]], axis=1)
                big = jnp.dot(both, jnp.concatenate([wide, fine], axis=0), preferred_element_type=jnp.float32)
                total = big[:rows] + big[rows:]
                for v in range(rows // SROW):
                    span = first * PROW // SROW + v
                    prods[span, o, 2 * a] = total[v * SROW : (v + 1) * SROW, :BLK]
                    prods[span, o, 2 * a + 1] = total[v * SROW : (v + 1) * SROW, BLK:]

        def some(i, carry):
            for j in range(unroll):
                one(i * unroll + j)
            return carry

        lax.fori_loop(0, ASLOT // unroll, some, 0)

    def gather(zz, o, spans, begin, end):
        base = o * (BLK // 2) + zz * BSLOT

        def some(i, carry):
            for j in range(CSZ):
                s = i * CSZ + j
                at = [tab_s[s, base + b] for b in range(BSLOT)]
                for v in spans:
                    terms = [prods[v, o, p] for p in at]
                    while len(terms) > 1:
                        terms = [x + w for x, w in zip(terms[::2], terms[1::2])]
                    acc[v, o, s] += terms[0]
            return carry

        lax.fori_loop(begin // CSZ, end // CSZ, some, 0)

    offset = (z + NY - y) % NY
    one_first = jnp.where(offset == 2, 1, 0)
    one_second = jnp.where((offset == 1) | (offset == 2), -1, 1)

    def near(k, carry):
        @pl.when(k == 1)
        def _():
            b_here(0, 2)
            b_done(0, 2)
            for j in (2, 3):
                from_left(2, j)
                from_right(2, j)

        @pl.when(k == 2)
        def _():
            b_here(1, 2)
            b_done(1, 2)
            a_step(3, 0)
            for j in (2, 3):
                a_right(2, j).start()
                a_left(2, j).start()
            take_b(0, 2)
            take_b(1, 2)

        third = -one_first - one_second
        by = jnp.where(k == 0, one_first, jnp.where(k == 1, one_second, jnp.where(k == 2, third, 14 - 4 * k)))
        zz = (z + NZ + by) % NZ
        multiply(zz, 0, PARTS, (0, 1))
        for o in (0, 1):
            gather(zz, o, range(SPANS), 0, CSLOT)
        return carry

    lax.fori_loop(0, 5, near, 0)
    from_left(3, 2)
    a_right(3, 2).start()
    from_right(3, 2)
    a_left(3, 2).start()

    def c_piece(v, o, j):
        return acc.at[v, o, pl.ds(j * CSZ, CSZ)]

    def c_landing(v, j):
        return crecv.at[v, pl.ds(j * CSZ, CSZ)]

    def send_c(v, j):
        return remote(c_piece(v, 1, j), c_landing(v, j), s_c.at[v, j], r_c.at[v, j], partner)

    def out_piece(v, j, which):
        return o_ref.at[pl.ds(j * CSZ, CSZ), 0, pl.ds(which * ROWS + v * SROW, SROW), :]

    def send_m(v, j):
        return remote(c_piece(v, 0, j), out_piece(v, j, half), s_m.at[v, j], r_m.at[v, j], mate)

    def store_o(v, j):
        return pltpu.make_async_copy(c_piece(v, 0, j), out_piece(v, j, half), s_o.at[v, j])

    def far(v, o):
        def one(i, carry):
            zz = (z + 3 + 2 * i) % NZ
            multiply(zz, 2 * v, 2, (o,))
            gather(zz, o, (v,), 0, CSLOT)
            return carry

        lax.fori_loop(0, 2, one, 0)

    def finish(v, j):
        landed(c_landing(v, j), r_c.at[v, j])

        def add(s, carry):
            acc[v, 0, s] += crecv[v, s]
            return carry

        lax.fori_loop(j * CSZ, (j + 1) * CSZ, add, 0)
        send_m(v, j).start()
        store_o(v, j).start()

    last = (z + 4) % NZ

    def give(v):
        from_left(4, 2 * v)
        from_right(4, 2 * v)
        multiply(last, 2 * v, 2, (1,))

        def one(j, carry):
            gather(last, 1, (v,), j * CSZ, (j + 1) * CSZ)
            send_c(v, j).start()
            return carry

        lax.fori_loop(0, CCH, one, 0)

    def keep(v):
        multiply(last, 2 * v, 2, (0,))
        gather(last, 0, (v,), 0, CSLOT)

    from_left(3, 1)
    from_right(3, 1)
    far(0, 1)
    give(0)
    far(0, 0)
    keep(0)
    finish(0, 0)
    from_left(3, 3)
    from_right(3, 3)
    far(1, 1)
    finish(0, 1)
    give(1)
    finish(0, 2)
    far(1, 0)
    finish(0, 3)
    keep(1)
    for j in range(CCH):
        finish(1, j)

    for v in range(SPANS):
        for j in range(CCH):
            landed(out_piece(v, j, 1 - half), r_m.at[v, j])
            store_o(v, j).wait()
            send_m(v, j).wait_send()
            send_c(v, j).wait_send()

    def end_ia(i, carry):
        send_ia(i).wait_send()
        return carry

    def end_ib(i, carry):
        pl.when(other_ib(i))(lambda: send_ib(i).wait_send())
        return carry

    lax.fori_loop(1, NZ, end_ia, 0)
    lax.fori_loop(0, 2 * NY, end_ib, 0)
    send_ic.wait_send()

    @pl.when(own)
    def _():
        for s in (0, 1):
            pl.when(q != s)(lambda: send_bd(0, s).wait_send())
            send_bd(1, s).wait_send()
            send_bd(3, s).wait_send()

    @pl.when(jnp.logical_not(own))
    def _():
        send_bp(0).wait_send()
        send_bp(1).wait_send()

    for o in (0, 1):
        b_next(o).wait_send()
        b_pass(o).wait_send()
        for i in range(NY):
            spread(o, b_slot(i), i * 2 + o).wait_send()

    def end_a(j, carry):
        for dist in range(3):
            a_right(dist, j).wait_send()
            a_left(dist, j).wait_send()

        @pl.when(j % 2 == 0)
        def _():
            a_right(3, j).wait_send()
            a_left(3, j).wait_send()

        return carry

    lax.fori_loop(0, PARTS, end_a, 0)


UNROLL = 8
ROUNDS = 3


def index_rows(a_index, b_index, c_index):
    def place(part, row, lane):
        rows, lanes = part.shape
        return lax.pad(part, jnp.int32(-1), ((row, 8 - row - rows, 0), (lane, BLK - lane - lanes, 0)))

    ours = jnp.maximum(place(a_index[:, :, 0], 0, 0), place(b_index[:, 0, :, 0], 2, 0))
    ours = jnp.maximum(ours, place(b_index[:, 1, :, 0], 2, BLK // 4))
    return jnp.maximum(ours, place(c_index[:, :, 0], 4, 0))


def local(a_blocks, a_index, b_blocks, b_index, c_index):
    dma = pltpu.SemaphoreType.DMA
    f32, bf16, i32 = jnp.float32, jnp.bfloat16, jnp.int32
    anywhere, outside = pl.BlockSpec(memory_space=pl.ANY), pl.BlockSpec(memory_space=pltpu.HBM)
    return pl.pallas_call(
        kernel,
        out_shape=jax.ShapeDtypeStruct((CSLOT, 1, BLK, BLK), f32),
        in_specs=[pl.BlockSpec(memory_space=pltpu.VMEM), outside, outside],
        out_specs=anywhere,
        scratch_shapes=[
            pltpu.VMEM((NZ, 8, BLK), i32),
            pltpu.VMEM((2 * NY, 8, BLK), i32),
            pltpu.VMEM((8, BLK), i32),
            pltpu.VMEM((3, CSLOT, BLK), i32),
            pltpu.VMEM((8, 2 * BLK), i32),
            pltpu.SMEM((CSLOT, BLK), i32),
            pltpu.SMEM((8, 2 * BLK), i32),
            pltpu.VMEM((NZ, PARTS, ASLOT, PROW, BLK), f32),
            pltpu.VMEM((2, NZ, BSLOT, BLK, BLK), f32),
            pltpu.VMEM((2, NZ, BSLOT, BLK, BLK), bf16),
            pltpu.VMEM((2, NZ, BSLOT, BLK, BLK), bf16),
            pltpu.VMEM((SPANS, 2, ZERO + 1, SROW, BLK), f32),
            pltpu.VMEM((SPANS, 2, CSLOT, SROW, BLK), f32),
            pltpu.VMEM((SPANS, CSLOT, SROW, BLK), f32),
            dma((NZ,)), dma((NZ,)), dma((2 * NY,)), dma((2 * NY,)), dma, dma, dma((2,)),
            dma((4, PARTS)), dma((4, PARTS)), dma((NZ, PARTS)), dma((PARTS,)),
            dma((NY, 2)), dma((2,)), dma((2,)), dma((2 * NY,)), dma((2, NZ)),
            dma((SPANS, CCH)), dma((SPANS, CCH)), dma((SPANS, CCH)), dma((SPANS, CCH)), dma((SPANS, CCH)),
            pltpu.SemaphoreType.REGULAR((ROUNDS,)),
        ],
        compiler_params=pltpu.CompilerParams(
            collective_id=0, has_side_effects=True, vmem_limit_bytes=36 * 1024 * 1024
        ),
        cost_estimate=pl.CostEstimate(flops=10**10, bytes_accessed=10**7, transcendentals=0),
    )(index_rows(a_index, b_index, c_index), a_blocks, b_blocks)


def solution(mesh):
    in_specs = (
        P("row", "col", None, None),
        P(None, "row", "col"),
        P(None, "row", "col", None, None),
        P(None, None, "row", "col"),
        P(None, "row", "col"),
    )
    out_specs = P("row", "col", None, None)
    return jax.shard_map(local, mesh=mesh, in_specs=in_specs, out_specs=out_specs, check_vma=False)
```

```python
import functools

import jax
import jax.numpy as jnp
from jax import lax
from jax.experimental import pallas as pl
from jax.experimental.pallas import tpu as pltpu
from jax.sharding import PartitionSpec as P

MESH = pl.DeviceIdType.MESH
NZ, NY = 8, 4
ASLOT, BSLOT, CSLOT, BLK = 24, 8, 32, 128
ROWS = BLK // 2
PARTS, PROW = 4, ROWS // 4
SPANS, SROW = 2, ROWS // 2
CCH, CSZ = 8, CSLOT // 8
UNROLL = 8
ROUNDS = 3
LANE_A = 32
ZERO = 2 * ASLOT


def kernel(
    idx_ref, a_ref, b_ref, o_ref,
    idx_a, idx_b, idx_c, tab_v, low_v, tab_s, low_s,
    abuf, bbuf, bhi, blo, prods, acc, crecv,
    s_ia, r_ia, s_ib, r_ib, s_ic, r_ic, s_tab,
    s_al, s_ar, r_a, s_loc, s_bd, s_bn, s_bf, s_bx, r_b, s_c, r_c, s_o, s_m, r_m, hello,
):
    r = lax.axis_index("row")
    c = lax.axis_index("col")
    d = lax.axis_index("depth")
    y, q = r // 2, r % 2
    z, h = c // 2, c % 2
    half = (h + d) % 2
    own = q == h
    role = (q + h) % 2
    b_col = z * 2 + q
    b_depth = (d + h + q) % 2
    partner = (r, z * 2 + 1 - h, 1 - d)
    mate = (r, c, 1 - d)
    twin = (y * 2 + 1 - q, c, d)
    up, down = (((y + 1) % NY) * 2 + q, c, d), (((y + 3) % NY) * 2 + q, c, d)
    right, left = (r, ((z + 1) % NZ) * 2 + h, d), (r, ((z + 7) % NZ) * 2 + h, d)

    def remote(src, dst, send, recv, device):
        return pltpu.make_async_remote_copy(
            src_ref=src, dst_ref=dst, send_sem=send, recv_sem=recv, device_id=device, device_id_type=MESH
        )

    def landed(ref, sem):
        pltpu.make_async_copy(ref, ref, sem).wait()

    barrier = pltpu.get_barrier_semaphore()
    near_by = [right, left, up, down, twin, partner, mate]
    near_by += [(((y + i) % NY) * 2 + 1 - q, c, d) for i in (1, 3)]
    near_by += [(y * 2 + 1 - q, z * 2 + 1 - h, 1 - d)]
    for device in near_by:
        pl.semaphore_signal(barrier, inc=1, device_id=device, device_id_type=MESH)
    pl.semaphore_wait(barrier, len(near_by))

    def send_bd(i, s):
        yy = (y + i) % NY
        return remote(b_ref.at[s, :, 0], bbuf.at[0, s * NY + y], s_bd.at[i, s], r_b.at[0, s * NY + y], (yy * 2 + s, c, d))

    def send_bp(s):
        return remote(
            b_ref.at[s, :, 0], bbuf.at[1, s * NY + y], s_bd.at[0, s], r_b.at[1, s * NY + y],
            (y * 2 + s, z * 2 + 1 - h, 1 - d),
        )

    local_b = pltpu.make_async_copy(b_ref.at[q, :, 0], bbuf.at[0, q * NY + y], r_b.at[0, q * NY + y])

    @pl.when(own)
    def _():
        for s in (0, 1):
            pl.when(q != s)(lambda: send_bd(0, s).start())
            send_bd(1, s).start()
            send_bd(3, s).start()
        local_b.start()

    @pl.when(jnp.logical_not(own))
    def _():
        send_bp(0).start()
        send_bp(1).start()

    def own_part(p):
        return a_ref.at[:, 0, pl.ds(half * ROWS + p * PROW, PROW), :]

    def part(zz, p):
        return abuf.at[zz, p]

    def turn(j):
        return j + 1 - 2 * (j % 2)

    def a_right(dist, j):
        zz = (z + NZ - dist) % NZ
        return remote(part(zz, j), part(zz, j), s_ar.at[dist, j], r_a.at[zz, j], right)

    def a_left(dist, j):
        zz, p = (z + dist) % NZ, turn(j)
        return remote(part(zz, p), part(zz, p), s_al.at[dist, j], r_a.at[zz, p], left)

    def from_left(dist, j):
        zz = (z + NZ - dist) % NZ
        landed(part(zz, j), r_a.at[zz, j])

    def from_right(dist, j):
        zz, p = (z + dist) % NZ, turn(j)
        landed(part(zz, p), r_a.at[zz, p])

    def local_a(p):
        return pltpu.make_async_copy(own_part(p), part(z, p), s_loc.at[p])

    def start_a(j, carry):
        p = turn(j)
        remote(own_part(j), part(z, j), s_ar.at[0, j], r_a.at[z, j], right).start()
        remote(own_part(p), part(z, p), s_al.at[0, j], r_a.at[z, p], left).start()
        local_a(j).start()
        return carry

    lax.fori_loop(0, PARTS, start_a, 0)

    for n in range(ROUNDS):
        for device in near_by:
            pl.semaphore_signal(hello.at[n], inc=1, device_id=device, device_id_type=MESH)
        pl.semaphore_wait(hello.at[n], len(near_by))

    def send_ia(i):
        return remote(idx_ref, idx_a.at[z], s_ia.at[i], r_ia.at[z], (r, ((z + i) % NZ) * 2 + h, d))

    def send_ib(i):
        yy, core = (y + i // 2) % NY, i % 2
        at = role * NY + y
        return remote(idx_ref, idx_b.at[at], s_ib.at[i], r_ib.at[at], (yy * 2 + core, b_col, b_depth))

    def other_ib(i):
        return jnp.logical_not(own & (i // 2 == 0) & (i % 2 == q))

    send_ic = remote(idx_ref, idx_c, s_ic, r_ic, partner)

    def start_ia(i, carry):
        send_ia(i).start()
        return carry

    def start_ib(i, carry):
        pl.when(other_ib(i))(lambda: send_ib(i).start())
        return carry

    lax.fori_loop(1, NZ, start_ia, 0)
    lax.fori_loop(0, 2 * NY, start_ib, 0)
    send_ic.start()
    idx_a[z] = idx_ref[...]

    @pl.when(own)
    def _():
        idx_b[y] = idx_ref[...]

    acc[...] = jnp.zeros_like(acc)
    for v in range(SPANS):
        for o in (0, 1):
            prods[v, o, ZERO] = jnp.zeros((SROW, BLK), jnp.float32)

    def tables():
        def wait_ia(i, carry):
            zz = (z + i) % NZ
            landed(idx_a.at[zz], r_ia.at[zz])
            return carry

        lax.fori_loop(1, NZ, wait_ia, 0)

        def wait_ib(i, carry):
            yy = (y + i) % NY
            landed(idx_b.at[NY + yy], r_ib.at[NY + yy])
            pl.when(jnp.logical_not(own & (i == 0)))(lambda: landed(idx_b.at[yy], r_ib.at[yy]))
            return carry

        lax.fori_loop(0, NY, wait_ib, 0)
        landed(idx_c, r_ic)

        a_sets = []
        for g in (0, 1):
            rolled = [pltpu.roll(idx_a[g * 4 + i] + 1, i * LANE_A, 1) if i else idx_a[g * 4] + 1 for i in range(4)]
            a_sets.append(rolled[0] + rolled[1] + (rolled[2] + rolled[3]))
        rolled = [pltpu.roll(idx_b[i] + 1, (i // NY) * (BLK // 2) + (i % NY) * BSLOT, 1) if i else idx_b[0] + 1 for i in range(2 * NY)]
        while len(rolled) > 1:
            rolled = [x + w for x, w in zip(rolled[::2], rolled[1::2])]
        b_key, b_to = rolled[0][2:3], rolled[0][3:4]
        a_in = jnp.concatenate([a_sets[0][1:2], a_sets[1][1:2]], axis=1)

        def column(row, count):
            wide = jnp.broadcast_to(row, (count, BLK))
            at = lax.broadcasted_iota(jnp.int32, (count, BLK), 0)
            lane = lax.broadcasted_iota(jnp.int32, (count, BLK), 1)
            return jnp.sum(jnp.where(at == lane, wide, 0), axis=1, keepdims=True)

        key_col = column(b_key, BLK)
        at = lax.broadcasted_iota(jnp.int32, (BLK, 2 * BLK), 0)
        match = (key_col == a_in) & (a_in > 0)
        low_v[...] = jnp.zeros_like(low_v)
        for o in (0, 1):
            mine = match & (at // (BLK // 2) == o)
            first = jnp.min(jnp.where(mine, at % BSLOT, BSLOT), axis=0, keepdims=True)
            last = jnp.max(jnp.where(mine, at % BSLOT, 0), axis=0, keepdims=True)
            low_v[2 * o : 2 * o + 1] = jnp.where(first == BSLOT, 0, first)
            low_v[2 * o + 1 : 2 * o + 2] = last
        at2 = at[:, :BLK]
        lane2 = lax.broadcasted_iota(jnp.int32, (BLK, BLK), 1)
        earlier = (key_col == b_key) & (at2 < lane2) & (at2 // (BLK // 2) == lane2 // (BLK // 2))
        second = jnp.max(jnp.where(earlier, 1, 0), axis=0, keepdims=True)
        row_col = jnp.concatenate([column(a_sets[g][0:1], BLK) for g in (0, 1)], axis=0)
        in_col = jnp.concatenate([column(a_sets[g][1:2], BLK) for g in (0, 1)], axis=0)
        slot = lax.broadcasted_iota(jnp.int32, (2 * BLK, BLK), 0) % LANE_A
        weight = jnp.where((in_col == b_key) & (in_col > 0), slot + 1, 0)
        lane3 = lax.broadcasted_iota(jnp.int32, (CSLOT, BLK), 1)
        mine_c, other_c = idx_ref[...] + 1, idx_c[...] + 1
        for i in (0, 1):
            tab_v[i] = jnp.where(
                lane3 < BLK // 2, column(mine_c[4 + i : 5 + i], CSLOT), column(other_c[4 + i : 5 + i], CSLOT)
            )

        def one_slot(s, carry):
            out_row, out_col = tab_v[0, pl.ds(s, 1)], tab_v[1, pl.ds(s, 1)]
            found = jnp.max(jnp.where(row_col == out_row, weight, 0), axis=0, keepdims=True)
            place = jnp.clip(2 * found - 2 + second, 0, ZERO)
            tab_v[2, pl.ds(s, 1)] = jnp.where((found > 0) & (out_col == b_to), place, ZERO)
            return carry

        lax.fori_loop(0, CSLOT, one_slot, 0)
        for copy in (tab_copy, low_copy):
            copy.start()

    tab_copy = pltpu.make_async_copy(tab_v.at[2], tab_s, s_tab.at[0])
    low_copy = pltpu.make_async_copy(low_v, low_s, s_tab.at[1])

    def spread(o, zz, slot):
        return remote(bbuf.at[o, zz], bbuf.at[o, zz], s_bx.at[slot], r_b.at[o, zz], twin)

    def split_b(o, zz):
        def one(i, carry):
            value = bbuf[o, zz, i]
            high = value.astype(jnp.bfloat16)
            bhi[o, zz, i] = high
            blo[o, zz, i] = (value - high.astype(jnp.float32)).astype(jnp.bfloat16)
            return carry

        lax.fori_loop(0, BSLOT, one, 0)

    def b_slot(i):
        return q * NY + (y + i) % NY

    def b_here(o, i):
        landed(bbuf.at[o, b_slot(i)], r_b.at[o, b_slot(i)])

    def b_next(way):
        zz = b_slot(0)
        return remote(bbuf.at[1, zz], bbuf.at[1, zz], s_bn.at[way], r_b.at[1, zz], (up, down)[way])

    def b_pass(o):
        zz = b_slot(3 if o == 0 else 1)
        return remote(bbuf.at[o, zz], bbuf.at[o, zz], s_bf.at[o], r_b.at[o, zz], (up, down)[o])

    def b_done(o, i):
        spread(o, b_slot(i), i * 2 + o).start()
        split_b(o, b_slot(i))

    def a_step(dist, j):
        from_left(dist, j)
        a_right(dist, j).start()
        from_right(dist, j)
        a_left(dist, j).start()

    a_step(1, 0)
    b_here(0, 0)
    b_done(0, 0)
    a_step(1, 1)
    b_here(1, 0)
    b_next(0).start()
    b_next(1).start()
    b_done(1, 0)
    a_step(1, 2)
    b_here(0, 3)
    b_pass(0).start()
    b_here(0, 1)
    b_done(0, 3)
    b_done(0, 1)
    a_step(1, 3)
    tables()
    b_here(1, 1)
    b_pass(1).start()
    b_here(1, 3)
    b_done(1, 1)
    b_done(1, 3)
    a_step(2, 0)

    def take_b(o, i):
        zz = (1 - q) * NY + (y + i) % NY
        landed(bbuf.at[o, zz], r_b.at[o, zz])
        split_b(o, zz)

    def take_near(k, carry):
        take_b(k // 3, (k % 3 + 3) % NY)
        return carry

    lax.fori_loop(0, 6, take_near, 0)
    a_step(2, 1)
    for p in range(PARTS):
        local_a(p).wait()
    tab_copy.wait()
    low_copy.wait()

    def multiply(zz, first, count, outs):
        rows = count * PROW
        unroll = UNROLL if len(outs) == 2 else UNROLL + UNROLL // 2

        def one(a):
            value = abuf[zz, first : first + count, a].reshape(rows, BLK)
            high = value.astype(jnp.bfloat16)
            low = (value - high.astype(jnp.float32)).astype(jnp.bfloat16)
            twice = [jnp.concatenate([part, part], axis=1) for part in (high, low)]
            both = jnp.concatenate(twice, axis=0)
            for o in outs:
                b0 = low_s[2 * o, zz * LANE_A + a]
                b1 = low_s[2 * o + 1, zz * LANE_A + a]
                wide = jnp.concatenate([bhi[o, zz, b0], bhi[o, zz, b1]], axis=1)
                fine = jnp.concatenate([blo[o, zz, b0], blo[o, zz, b1]], axis=1)
                big = jnp.dot(both, jnp.concatenate([wide, fine], axis=0), preferred_element_type=jnp.float32)
                total = big[:rows] + big[rows:]
                for v in range(rows // SROW):
                    span = first * PROW // SROW + v
                    prods[span, o, 2 * a] = total[v * SROW : (v + 1) * SROW, :BLK]
                    prods[span, o, 2 * a + 1] = total[v * SROW : (v + 1) * SROW, BLK:]

        def some(i, carry):
            for j in range(unroll):
                one(i * unroll + j)
            return carry

        lax.fori_loop(0, ASLOT // unroll, some, 0)

    def gather(zz, o, spans, begin, end, unroll=UNROLL):
        base = o * (BLK // 2) + zz * BSLOT

        def some(i, carry):
            for j in range(unroll):
                s = i * unroll + j
                at = [tab_s[s, base + b] for b in range(BSLOT)]
                for v in spans:
                    terms = [prods[v, o, p] for p in at]
                    while len(terms) > 1:
                        terms = [x + w for x, w in zip(terms[::2], terms[1::2])]
                    acc[v, o, s] += terms[0]
            return carry

        lax.fori_loop(begin // unroll, end // unroll, some, 0)

    offset = (z + NY - y) % NY
    one_first = jnp.where(offset == 2, 1, 0)
    one_second = jnp.where((offset == 1) | (offset == 2), -1, 1)

    def near(k, carry):
        @pl.when(k == 1)
        def _():
            b_here(0, 2)
            b_done(0, 2)
            for j in (2, 3):
                from_left(2, j)
                from_right(2, j)

        @pl.when(k == 2)
        def _():
            b_here(1, 2)
            b_done(1, 2)
            a_step(3, 0)
            for j in (2, 3):
                a_right(2, j).start()
                a_left(2, j).start()
            take_b(0, 2)
            take_b(1, 2)

        third = -one_first - one_second
        by = jnp.where(k == 0, one_first, jnp.where(k == 1, one_second, jnp.where(k == 2, third, 14 - 4 * k)))
        zz = (z + NZ + by) % NZ
        multiply(zz, 0, PARTS, (0, 1))
        for o in (0, 1):
            gather(zz, o, range(SPANS), 0, CSLOT)
        return carry

    lax.fori_loop(0, 5, near, 0)
    from_left(3, 2)
    a_right(3, 2).start()
    from_right(3, 2)
    a_left(3, 2).start()

    def c_piece(v, o, j):
        return acc.at[v, o, pl.ds(j * CSZ, CSZ)]

    def c_landing(v, j):
        return crecv.at[v, pl.ds(j * CSZ, CSZ)]

    def send_c(v, j):
        return remote(c_piece(v, 1, j), c_landing(v, j), s_c.at[v, j], r_c.at[v, j], partner)

    def out_piece(v, j, which):
        return o_ref.at[pl.ds(j * CSZ, CSZ), 0, pl.ds(which * ROWS + v * SROW, SROW), :]

    def send_m(v, j):
        return remote(c_piece(v, 0, j), out_piece(v, j, half), s_m.at[v, j], r_m.at[v, j], mate)

    def store_o(v, j):
        return pltpu.make_async_copy(c_piece(v, 0, j), out_piece(v, j, half), s_o.at[v, j])

    def far(v, o):
        def one(i, carry):
            zz = (z + 3 + 2 * i) % NZ
            multiply(zz, 2 * v, 2, (o,))
            gather(zz, o, (v,), 0, CSLOT)
            return carry

        lax.fori_loop(0, 2, one, 0)

    def finish(v, j):
        landed(c_landing(v, j), r_c.at[v, j])

        def add(s, carry):
            acc[v, 0, s] += crecv[v, s]
            return carry

        lax.fori_loop(j * CSZ, (j + 1) * CSZ, add, 0)
        send_m(v, j).start()
        store_o(v, j).start()

    last = (z + 4) % NZ

    def give(v):
        from_left(4, 2 * v)
        from_right(4, 2 * v)
        multiply(last, 2 * v, 2, (1,))

        def one(j, carry):
            gather(last, 1, (v,), j * CSZ, (j + 1) * CSZ, CSZ)
            send_c(v, j).start()
            return carry

        lax.fori_loop(0, CCH, one, 0)

    def keep(v):
        multiply(last, 2 * v, 2, (0,))
        gather(last, 0, (v,), 0, CSLOT)

    from_left(3, 1)
    from_right(3, 1)
    far(0, 1)
    give(0)
    far(0, 0)
    keep(0)
    finish(0, 0)
    finish(0, 1)
    from_left(3, 3)
    from_right(3, 3)
    far(1, 1)
    finish(0, 2)
    finish(0, 3)
    give(1)
    finish(0, 4)
    finish(0, 5)
    far(1, 0)
    finish(0, 6)
    finish(0, 7)
    keep(1)
    for j in range(CCH):
        finish(1, j)

    for v in range(SPANS):
        for j in range(CCH):
            landed(out_piece(v, j, 1 - half), r_m.at[v, j])
            store_o(v, j).wait()
            send_m(v, j).wait_send()
            send_c(v, j).wait_send()

    def end_ia(i, carry):
        send_ia(i).wait_send()
        return carry

    def end_ib(i, carry):
        pl.when(other_ib(i))(lambda: send_ib(i).wait_send())
        return carry

    lax.fori_loop(1, NZ, end_ia, 0)
    lax.fori_loop(0, 2 * NY, end_ib, 0)
    send_ic.wait_send()

    @pl.when(own)
    def _():
        for s in (0, 1):
            pl.when(q != s)(lambda: send_bd(0, s).wait_send())
            send_bd(1, s).wait_send()
            send_bd(3, s).wait_send()

    @pl.when(jnp.logical_not(own))
    def _():
        send_bp(0).wait_send()
        send_bp(1).wait_send()

    for o in (0, 1):
        b_next(o).wait_send()
        b_pass(o).wait_send()
        for i in range(NY):
            spread(o, b_slot(i), i * 2 + o).wait_send()

    def end_a(j, carry):
        for dist in range(3):
            a_right(dist, j).wait_send()
            a_left(dist, j).wait_send()

        @pl.when(j % 2 == 0)
        def _():
            a_right(3, j).wait_send()
            a_left(3, j).wait_send()

        return carry

    lax.fori_loop(0, PARTS, end_a, 0)


def index_rows(a_index, b_index, c_index):
    def place(part, row, lane):
        rows, lanes = part.shape
        return lax.pad(part, jnp.int32(-1), ((row, 8 - row - rows, 0), (lane, BLK - lane - lanes, 0)))

    ours = jnp.maximum(place(a_index[:, :, 0], 0, 0), place(b_index[:, 0, :, 0], 2, 0))
    ours = jnp.maximum(ours, place(b_index[:, 1, :, 0], 2, BLK // 4))
    return jnp.maximum(ours, place(c_index[:, :, 0], 4, 0))


def local(a_blocks, a_index, b_blocks, b_index, c_index):
    dma = pltpu.SemaphoreType.DMA
    f32, bf16, i32 = jnp.float32, jnp.bfloat16, jnp.int32
    anywhere, outside = pl.BlockSpec(memory_space=pl.ANY), pl.BlockSpec(memory_space=pltpu.HBM)
    return pl.pallas_call(
        kernel,
        out_shape=jax.ShapeDtypeStruct((CSLOT, 1, BLK, BLK), f32),
        in_specs=[pl.BlockSpec(memory_space=pltpu.VMEM), outside, outside],
        out_specs=anywhere,
        scratch_shapes=[
            pltpu.VMEM((NZ, 8, BLK), i32),
            pltpu.VMEM((2 * NY, 8, BLK), i32),
            pltpu.VMEM((8, BLK), i32),
            pltpu.VMEM((3, CSLOT, BLK), i32),
            pltpu.VMEM((8, 2 * BLK), i32),
            pltpu.SMEM((CSLOT, BLK), i32),
            pltpu.SMEM((8, 2 * BLK), i32),
            pltpu.VMEM((NZ, PARTS, ASLOT, PROW, BLK), f32),
            pltpu.VMEM((2, NZ, BSLOT, BLK, BLK), f32),
            pltpu.VMEM((2, NZ, BSLOT, BLK, BLK), bf16),
            pltpu.VMEM((2, NZ, BSLOT, BLK, BLK), bf16),
            pltpu.VMEM((SPANS, 2, ZERO + 1, SROW, BLK), f32),
            pltpu.VMEM((SPANS, 2, CSLOT, SROW, BLK), f32),
            pltpu.VMEM((SPANS, CSLOT, SROW, BLK), f32),
            dma((NZ,)), dma((NZ,)), dma((2 * NY,)), dma((2 * NY,)), dma, dma, dma((2,)),
            dma((4, PARTS)), dma((4, PARTS)), dma((NZ, PARTS)), dma((PARTS,)),
            dma((NY, 2)), dma((2,)), dma((2,)), dma((2 * NY,)), dma((2, NZ)),
            dma((SPANS, CCH)), dma((SPANS, CCH)), dma((SPANS, CCH)), dma((SPANS, CCH)), dma((SPANS, CCH)),
            pltpu.SemaphoreType.REGULAR((ROUNDS,)),
        ],
        compiler_params=pltpu.CompilerParams(
            collective_id=0, has_side_effects=True, vmem_limit_bytes=36 * 1024 * 1024
        ),
        cost_estimate=pl.CostEstimate(flops=10**10, bytes_accessed=10**7, transcendentals=0),
    )(index_rows(a_index, b_index, c_index), a_blocks, b_blocks)


def solution(mesh):
    in_specs = (
        P("row", "col", None, None),
        P(None, "row", "col"),
        P(None, "row", "col", None, None),
        P(None, None, "row", "col"),
        P(None, "row", "col"),
    )
    out_specs = P("row", "col", None, None)
    return jax.shard_map(local, mesh=mesh, in_specs=in_specs, out_specs=out_specs, check_vma=False)
```
